32 devices in a mesh: ctx: 16 (over z, x, core), exp: 2 (over y).
Axes of the slice: x: 2, y: 2, z: 4, core: 2. Of those that a mesh axis runs over, the one named last changes fastest.
Arguments:
- queries: bfloat16 [128, 73728], P(('ctx', 'exp')), may hold values from -24 to 24
- latents: bfloat16 [1280, 576], P('ctx'), may hold values from -6 to 6
- offsets: int32 [32], P(('ctx', 'exp')), may hold values from 1152 to 1276, as said below
- moe_input: bfloat16 [64, 5120], P('exp', 'ctx'), may hold values from -6 to 6
- routes: int32 [64, 6], P('exp'), may hold values from 0 to 15, all different within a row; in each aligned block of 32 rows (0 to 31, 32 to 63, ...) at most 16 rows name the same one
- gate_values: float32 [64, 6], P('exp'), may hold values from 0.05 to 0.45
- w_gate: bfloat16 [16, 5120, 1536], P('exp', 'ctx'), may hold values from -0.078125 to 0.078125
- w_up: bfloat16 [16, 5120, 1536], P('exp', 'ctx'), may hold values from -0.078125 to 0.078125
- w_down: bfloat16 [16, 1536, 5120], P('exp', None, 'ctx'), may hold values from -0.15625 to 0.15625
Outputs:
- attention_out: bfloat16 [128, 65536], P(('ctx', 'exp'))
- moe_output: bfloat16 [64, 5120], P('exp', 'ctx')
The draws below stay inside these ranges and needn't reach their ends.
Inputs may be any that keep to these rules, and one draw needn't show every extreme that they name: `offsets`: the query blocks start at distinct positions 1152 + k * 4, one block for each k. `routes`: each row names 6 different experts; the 32 rows of one index of exp name no expert more than 16 times, and in every draw some expert is named exactly 16 times there.
All inputs are finite; a program needn't handle non-finite values.
Results may differ from the reference program's by a relative error of at most 0.0075.
Values may be sent and summed in bfloat16 or wider, within the bound.
A program may use at most 64 MiB of HBM per device.

```python
import math
import jax
import jax.numpy as jnp
import numpy as np
from jax import lax

D = 5120
FF = 1536
H = 128
LAT = 512
ROPE = 64
TOPK = 6
EXPERTS = 16
QD = 4
MT = 32
CAP = 16
STRETCH = 128
CTX = 1280
MTOK = 64


def draw_latents(key, part):
    base_key = jax.random.fold_in(key, 13)
    values = jnp.clip(jax.random.normal(base_key, (CTX, LAT + ROPE), jnp.float32), -6.0, 6.0)
    return values.astype(jnp.bfloat16)


def draw_queries(key, part):
    base_key = jax.random.fold_in(key, 11)
    values = jnp.clip(1.15 * jax.random.normal(base_key, (STRETCH * H, LAT + ROPE), jnp.float32), -6.9, 6.9)
    return values.reshape(STRETCH, H * (LAT + ROPE)).astype(jnp.bfloat16)


def draw_offsets(key, part):
    blocks = STRETCH // QD
    ordering = jax.random.permutation(jax.random.fold_in(key, 17), blocks)
    return (CTX - STRETCH + ordering.astype(jnp.int32) * QD).astype(jnp.int32)


def level_of(key, extent, shards, least, largest):
    gain = 1.0
    for axis_at, shards_of in shards:
        steps = jax.random.uniform(jax.random.fold_in(jax.random.fold_in(key, 6), axis_at), (shards_of,), jnp.float32, least / len(shards), largest / len(shards))
        gain = gain * jnp.repeat(jnp.exp(steps), extent[axis_at] // shards_of).reshape((-1,) + (1,) * (len(extent) - 1 - axis_at))
    return gain


def deal_out(rng, own, number, rows, amount, top, most, lean):
    order = jax.random.permutation(rng, amount)
    heavy_load, ordinary = load_shares(amount, rows * top, most, lean, True), load_shares(amount, rows * top, most, lean, False)
    places = jnp.arange(amount)

    def named(tallies, offset_by):
        used = int((tallies > 0).sum())
        fixed = max(1, used // 4)
        passed = fixed + (places - fixed + offset_by * (used - fixed)) % max(1, amount - fixed)
        return jnp.zeros((amount,), jnp.int32).at[order[jnp.where(places < fixed, places, passed)]].set(jnp.asarray(tallies, jnp.int32))

    tallies = jnp.where(number % 4 == 0, named(heavy_load, number // 4), named(ordinary, number - number // 4 - 1))
    mixed = jax.random.permutation(jax.random.fold_in(own, 3), amount)
    giver, receiver = mixed[0:amount // 2 * 2:2], mixed[1:amount // 2 * 2:2]
    room = jnp.minimum(tallies[giver] - 1, most - tallies[receiver]) // 2
    room = jnp.where((giver == order[0]) | (receiver == order[0]) | (tallies[receiver] == 0), 0, jnp.maximum(room, 0))
    passed = jax.random.randint(jax.random.fold_in(own, 4), (amount // 2,), 0, 1 << 20) % (room + 1)
    tallies = tallies.at[giver].add(-passed).at[receiver].add(passed)
    items = jnp.searchsorted(jnp.cumsum(tallies), jnp.arange(rows * top), side="right").astype(jnp.int32)
    table = items.reshape(top, rows).T
    table = table[jax.random.permutation(jax.random.fold_in(own, 1), rows)]
    offset_by = jax.random.randint(jax.random.fold_in(own, 2), (rows, 1), 0, top)
    return jnp.take_along_axis(table, (jnp.arange(top)[None, :] + offset_by) % top, axis=1)


def load_shares(count, total, bound, skew, full):
    portions = [(1 << 20) // math.isqrt(rank ** skew) + 1 for rank in range(1, count + 1)]
    largest = bound if full else min(bound, max(-(-total // count), total * portions[0] // sum(portions)))
    least = 1 if total - largest >= count - 1 else 0
    counts, spare = [largest] + [least] * (count - 1), total - largest - least * (count - 1)
    while spare > 0:
        candidates = [i for i in range(1, count) if counts[i] < largest] or [i for i in range(1, count) if counts[i] < bound]
        whole, remaining = sum([portions[i] for i in candidates]), spare
        for i in candidates:
            addition = min(bound - counts[i], max(1, remaining * portions[i] // whole), spare)
            counts[i] = counts[i] + addition
            spare = spare - addition
    return np.array(counts)


def centred(rng, dims, scale, most, pieces=(), held_as=jnp.bfloat16):
    drawn = scale * jax.random.normal(rng, dims, jnp.float32)
    if pieces:
        drawn = drawn * level_of(rng, dims, pieces, -0.22, 0.18)
    return jnp.clip(drawn, -most, most).astype(held_as)


def setup_inputs(seed: int = 0) -> dict:
    arg_keys = jax.random.split(jax.random.key(seed), 10)
    queries = draw_queries(jax.random.fold_in(arg_keys[9], 71), 0)
    latents = draw_latents(jax.random.fold_in(arg_keys[9], 71), 0)
    offsets = draw_offsets(jax.random.fold_in(arg_keys[9], 71), 0)
    moe_input = centred(arg_keys[3], (MTOK, D), 1.0, 6.0, ((0, 2), (1, 16)))
    routes_keys = jax.random.split(jax.random.fold_in(arg_keys[4], 1), MTOK // MT)
    routes_turns = jax.random.permutation(jax.random.fold_in(arg_keys[4], 3), MTOK // MT)
    routes = jax.vmap(lambda own, number: deal_out(jax.random.fold_in(arg_keys[4], 2), own, number, MT, EXPERTS, TOPK, CAP, 2))(routes_keys, routes_turns).reshape((MTOK, TOPK))
    gate_values = jnp.clip(0.05 + 0.39999999 * jax.random.uniform(arg_keys[5], (MTOK, TOPK), jnp.float32) ** level_of(arg_keys[5], (MTOK, TOPK), ((0, 2),), -0.2, 0.2), 0.05, 0.45)
    w_gate = centred(arg_keys[6], (EXPERTS, D, FF), D ** -0.5, 0.078125, ((0, 2), (1, 16)))
    w_up = centred(arg_keys[7], (EXPERTS, D, FF), D ** -0.5, 0.078125, ((0, 2), (1, 16)))
    w_down = centred(arg_keys[8], (EXPERTS, FF, D), FF ** -0.5, 0.15625, ((0, 2), (2, 16)))
    return dict(queries=queries, latents=latents, offsets=offsets, moe_input=moe_input, routes=routes, gate_values=gate_values, w_gate=w_gate, w_up=w_up, w_down=w_down)


softmax_scale = 192.0 ** -0.5


def attend_group(query_group, positions, latents, key_pos):
    scores = jnp.dot(query_group, latents.T, preferred_element_type=jnp.float32) * softmax_scale
    scores = jnp.where(key_pos[None, :] <= positions[:, None], scores, -jnp.inf)
    row_max = jnp.max(scores, axis=1, keepdims=True)
    weights = jnp.exp(scores - row_max)
    denominator = jnp.sum(weights, axis=1, keepdims=True)
    rounded = weights.astype(jnp.bfloat16)
    mixed = jnp.dot(rounded, latents[:, :LAT], preferred_element_type=jnp.float32)
    return (mixed / denominator).astype(jnp.bfloat16)


def reference(queries, latents, offsets, moe_input, routes, gate_values, w_gate, w_up, w_down):
    token_ids = jnp.arange(STRETCH, dtype=jnp.int32)
    positions = offsets[token_ids // QD] + token_ids % QD
    key_pos = jnp.arange(CTX, dtype=jnp.int32)
    grouped = queries.reshape(STRETCH // 8, 8 * H, LAT + ROPE)
    pos_rows = jnp.repeat(positions, H).reshape(STRETCH // 8, 8 * H)

    def one_group(inputs):
        return attend_group(inputs[0], inputs[1], latents, key_pos)

    mixed = lax.map(one_group, (grouped, pos_rows))
    attention_out = mixed.reshape(STRETCH, H * LAT)

    def expert_out(expert_index):
        gate_act = jnp.dot(moe_input, w_gate[expert_index], preferred_element_type=jnp.float32)
        up_act = jnp.dot(moe_input, w_up[expert_index], preferred_element_type=jnp.float32)
        hidden = (jax.nn.silu(gate_act) * up_act).astype(jnp.bfloat16)
        return jnp.dot(hidden, w_down[expert_index], preferred_element_type=jnp.float32).astype(jnp.bfloat16)

    all_experts = lax.map(expert_out, jnp.arange(EXPERTS, dtype=jnp.int32))
    picked = all_experts[routes, jnp.arange(MTOK, dtype=jnp.int32)[:, None]]
    moe_output = jnp.sum(picked.astype(jnp.float32) * gate_values[:, :, None], axis=1).astype(jnp.bfloat16)
    return (attention_out, moe_output)
```

```python
import functools

import jax
import jax.numpy as jnp
from jax import lax
from jax.experimental import pallas as pl
from jax.experimental.pallas import tpu as pltpu
from jax.sharding import PartitionSpec as P

H = 128
LAT = 512
ROPE = 64
TOPK = 6
EXPERTS = 16
CAP = 16
MESH = pl.DeviceIdType.MESH

softmax_scale = 192.0 ** (-0.5)


def attend_kernel(offset_ref, query_ref, key_ref, out_ref):
    keys = key_ref[...]
    values = key_ref[:, :LAT]
    key_pos = lax.broadcasted_iota(jnp.int32, (1, keys.shape[0]), 1)

    @pl.loop(0, query_ref.shape[0] // H)
    def _(token):
        rows = pl.ds(pl.multiple_of(token * H, H), H)
        scores = (
            lax.dot_general(
                query_ref[rows, :], keys, (((1,), (1,)), ((), ())), preferred_element_type=jnp.float32
            )
            * softmax_scale
        )
        scores = jnp.where(key_pos <= offset_ref[0] + token, scores, -jnp.inf)
        weights = jnp.exp(scores - jnp.max(scores, axis=1, keepdims=True))
        denominator = jnp.sum(weights, axis=1, keepdims=True)
        mixed = jnp.dot(weights.astype(jnp.bfloat16), values, preferred_element_type=jnp.float32)
        out_ref[rows, :] = (mixed / denominator).astype(out_ref.dtype)


def attend(queries, every_key, offsets):
    rows = queries.shape[0] * H
    out = pl.pallas_call(
        attend_kernel,
        out_shape=jax.ShapeDtypeStruct((rows, LAT), jnp.bfloat16),
        in_specs=[
            pl.BlockSpec(memory_space=pltpu.SMEM),
            pl.BlockSpec(memory_space=pltpu.VMEM),
            pl.BlockSpec(memory_space=pltpu.VMEM),
        ],
        out_specs=pl.BlockSpec(memory_space=pltpu.VMEM),
        compiler_params=pltpu.CompilerParams(vmem_limit_bytes=32 * 2**20),
        cost_estimate=pl.CostEstimate(
            flops=2 * rows * every_key.shape[0] * (2 * LAT + ROPE),
            bytes_accessed=rows * (2 * LAT + ROPE) * 2 + every_key.size * 2,
            transcendentals=rows * every_key.shape[0],
        ),
        name="attend",
    )(offsets, queries.reshape(rows, LAT + ROPE), every_key)
    return out.reshape(queries.shape[0], H * LAT)


def expert_kernel(
    n, owners,
    table_ref, tokens_ref, gate_hbm, up_hbm, down_hbm, out_ref,
    gate_w, up_w, down_w, w_sem,
    tables, tokens, t_ssem, t_rsem, x_rows,
    keep, core_send, core_recv, c_ssem, c_rsem,
    side_send, side_recv, s_ssem, s_rsem,
    far_send, far_recv, own, f_ssem, f_rsem,
    hidden, hz_ssem, hz_rsem, hx_ssem, hx_rsem, hc_ssem, hc_rsem,
    result, back_send, back_recv, b_ssem, b_rsem,
):
    held = gate_hbm.shape[0]
    ff = gate_hbm.shape[2]
    count = tokens_ref.shape[0]
    rows = owners * CAP
    half = rows // 2
    pairs = held // 2
    nz = n // 4
    subs = nz // pairs
    row_blocks = half // 16
    col_blocks = subs // row_blocks
    width = ff // col_blocks

    ctx = lax.axis_index("ctx")
    exp = lax.axis_index("exp")
    core = lax.rem(ctx, 2)
    side = lax.rem(ctx // 2, 2)
    far = ctx // 4
    sibling = (ctx + 1 - 2 * core, exp)
    beside = (ctx + 2 - 4 * side, exp)

    def at_far(index):
        return (index * 4 + side * 2 + core, exp)

    def far_of(step):
        return lax.rem(far + step, nz)

    def owner_of(step):
        return lax.rem(exp + step, owners)

    pair_of = [lax.rem(far // subs + 1 + i, pairs) for i in range(pairs)]
    weight_copies = {}
    for i in range(pairs):
        for j in range(2):
            expert = pair_of[i] * 2 + (1 - side if j == 0 else side)
            weight_copies[i, j] = [
                pltpu.make_async_copy(hbm.at[expert], vmem.at[expert], w_sem.at[k, i, j])
                for k, (hbm, vmem) in enumerate(((gate_hbm, gate_w), (up_hbm, up_w)))
            ]
            for copy in weight_copies[i, j]:
                copy.start()
    down_order = [(d, j) for d in range(pairs) for j in range(2)]
    down_expert = {}
    down_copies = {}
    for d, j in down_order:
        expert = lax.rem(far // subs + d, pairs) * 2 + (side if j == 0 else 1 - side)
        down_expert[d, j] = expert
        down_copies[d, j] = pltpu.make_async_copy(
            down_hbm.at[expert], down_w.at[expert], w_sem.at[2, d, j]
        )
        down_copies[d, j].start()

    barrier = pltpu.get_barrier_semaphore()
    greeted = [sibling, beside]
    greeted += [at_far(far_of(k)) for k in range(1, nz)]
    greeted += [(ctx, owner_of(k)) for k in range(1, owners)]
    for device in greeted:
        pl.semaphore_signal(barrier, inc=1, device_id=device, device_id_type=MESH)
    pl.semaphore_wait(barrier, len(greeted))

    sent = []

    def send(src, dst, ssem, rsem, device):
        copy = pltpu.make_async_remote_copy(
            src_ref=src, dst_ref=dst, send_sem=ssem, recv_sem=rsem,
            device_id=device, device_id_type=MESH,
        )
        copy.start()
        sent.append(copy)

    def arrived(dst, sem):
        pltpu.make_async_remote_copy(
            src_ref=dst, dst_ref=dst, send_sem=sem, recv_sem=sem,
            device_id=sibling, device_id_type=MESH,
        ).wait_recv()

    for k in range(1, owners):
        device = (ctx, owner_of(k))
        send(table_ref, tables.at[exp], t_ssem.at[0, k], t_rsem.at[0, exp], device)
        send(tokens_ref, tokens.at[exp], t_ssem.at[1, k], t_rsem.at[1, exp], device)

    first = exp * held
    expert_ids = (lax.broadcasted_iota(jnp.int32, (held, count), 0) + first).astype(jnp.float32)
    earlier = (
        lax.broadcasted_iota(jnp.int32, (count, count), 0)
        < lax.broadcasted_iota(jnp.int32, (count, count), 1)
    ).astype(jnp.bfloat16)
    slots = lax.broadcasted_iota(jnp.int32, (held, CAP, count), 1).astype(jnp.float32)

    def placement(table):
        named = jnp.zeros((held, count), jnp.float32)
        gates = jnp.zeros((held, count), jnp.float32)
        for k in range(TOPK):
            hit = table[k : k + 1, :count] == expert_ids
            named = jnp.where(hit, 1.0, named)
            gates = jnp.where(hit, table[8 + k : 9 + k, :count], gates)
        rank = jnp.dot(named.astype(jnp.bfloat16), earlier, preferred_element_type=jnp.float32)
        rank = jnp.where(named > 0.5, rank, -1.0)
        picked = rank[:, None, :] == slots
        chosen = jnp.where(picked, 1.0, 0.0).reshape(held * CAP, count)
        weighted = jnp.where(picked, gates[:, None, :], 0.0).reshape(held * CAP, count)
        return chosen.astype(jnp.bfloat16), weighted

    def place(table, values, owner):
        chosen, weighted = placement(table)
        placed = jnp.dot(chosen, values, preferred_element_type=jnp.float32).astype(jnp.bfloat16)
        for e in range(held):
            x_rows[e, pl.ds(pl.multiple_of(owner * CAP, CAP), CAP), :] = placed[e * CAP : (e + 1) * CAP]
        return weighted

    weighted_of = {0: place(table_ref[...], tokens_ref[...], exp)}
    for k in range(1, owners):
        owner = owner_of(k)
        arrived(tables.at[owner], t_rsem.at[0, owner])
        arrived(tokens.at[owner], t_rsem.at[1, owner])
        weighted_of[k] = place(tables[owner], tokens[owner], owner)

    mine = pl.ds(pl.multiple_of(core * half, 16), half)
    other = pl.ds(pl.multiple_of((1 - core) * half, 16), half)

    def multiply(i):
        for j in range(2):
            expert = pair_of[i] * 2 + (1 - side if j == 0 else side)
            for k, weight in ((0, gate_w), (1, up_w)):
                weight_copies[i, j][k].wait()
                columns = slice(k * ff, (k + 1) * ff)
                held_w = weight[expert]
                core_send[i, j, :, columns] = jnp.dot(
                    x_rows[expert, other, :], held_w, preferred_element_type=jnp.float32
                ).astype(jnp.bfloat16)
                keep[i, j, :, columns] = jnp.dot(
                    x_rows[expert, mine, :], held_w, preferred_element_type=jnp.float32
                )
            send(core_send.at[i, j], core_recv.at[i, j], c_ssem.at[i, j], c_rsem.at[i, j], sibling)

    def to_side(i):
        arrived(core_recv.at[i, 0], c_rsem.at[i, 0])
        side_send[i] = (keep[i, 0] + core_recv[i, 0].astype(jnp.float32)).astype(jnp.bfloat16)
        send(side_send.at[i], side_recv.at[i], s_ssem.at[i], s_rsem.at[i], beside)

    def block(i, sub):
        row = lax.rem(sub, row_blocks)
        return i, row, sub // row_blocks

    def to_far(i):
        arrived(core_recv.at[i, 1], c_rsem.at[i, 1])
        arrived(side_recv.at[i], s_rsem.at[i])
        total = (
            keep[i, 1] + core_recv[i, 1].astype(jnp.float32) + side_recv[i].astype(jnp.float32)
        )
        for r in range(row_blocks):
            for c in range(col_blocks):
                for k in range(2):
                    piece = total[r * 16 : r * 16 + 16, k * ff + c * width : k * ff + (c + 1) * width]
                    at = c * row_blocks + r
                    far_send[i, at, :, k * width : (k + 1) * width] = piece.astype(jnp.bfloat16)
                    if i == pairs - 1:
                        own[at, :, k * width : (k + 1) * width] = piece
        my_sub = lax.rem(far, subs)
        for s in range(subs if i < pairs - 1 else subs - 1):
            sub = lax.rem(my_sub + 1 + s, subs)
            dest = pair_of[i] * subs + sub
            send(
                far_send.at[i, sub], far_recv.at[far], f_ssem.at[i, s], f_rsem.at[far], at_far(dest)
            )

    for t in range(pairs + 2):
        if t < pairs:
            multiply(t)
        if 0 <= t - 1 < pairs:
            to_side(t - 1)
        if 0 <= t - 2 < pairs:
            to_far(t - 2)

    total = own[lax.rem(far, subs)]
    for k in range(1, nz):
        sender = far_of(nz - k)
        arrived(far_recv.at[sender], f_rsem.at[sender])
        total = total + far_recv[sender].astype(jnp.float32)
    gate, up = total[:, :width], total[:, width:]
    hidden[far, side, core] = (gate / (1.0 + jnp.exp(-gate)) * up).astype(jnp.bfloat16)

    def pass_on(where, slot_side, ssems, rsems, device):
        here = hidden.at[where, slot_side, core]
        send(here, here, ssems, rsems, device)

    mine_block = hidden.at[far, side, core]
    for k in range(1, nz):
        send(mine_block, mine_block, hz_ssem.at[k], hz_rsem.at[far], at_far(far_of(k)))
    for k in range(nz):
        where = far_of(nz - k) if k else far
        if k:
            arrived(hidden.at[where, side, core], hz_rsem.at[where])
        pass_on(where, side, hx_ssem.at[k], hx_rsem.at[where], beside)
        pass_on(where, side, hc_ssem.at[0, k], hc_rsem.at[0, where], sibling)
    for k in range(nz):
        where = far_of(nz - k) if k else far
        arrived(hidden.at[where, 1 - side, core], hx_rsem.at[where])
        pass_on(where, 1 - side, hc_ssem.at[1, k], hc_rsem.at[1, where], sibling)

    for j in range(2):
        slot_side = side if j == 0 else 1 - side
        for d in range(pairs):
            expert = down_expert[d, j]
            pair = lax.rem(far // subs + d, pairs)
            for s in range(subs):
                where = pair * subs + s
                arrived(hidden.at[where, slot_side, 1 - core], hc_rsem.at[j, where])
            strips = []
            for c in range(2):
                for r in range(row_blocks):
                    strips.append(
                        jnp.concatenate(
                            [
                                hidden[pair * subs + q * row_blocks + r, slot_side, c]
                                for q in range(col_blocks)
                            ],
                            axis=1,
                        )
                    )
            down_copies[d, j].wait()
            made = jnp.dot(
                jnp.concatenate(strips, axis=0), down_w[expert], preferred_element_type=jnp.float32
            ).astype(jnp.bfloat16)
            for s in range(owners):
                result[s, pl.ds(pl.multiple_of(expert * CAP, CAP), CAP), :] = made[
                    s * CAP : (s + 1) * CAP
                ]

    def combine(k):
        weighted = weighted_of[k]
        high = weighted.astype(jnp.bfloat16)
        rest = weighted - high.astype(jnp.float32)
        middle = rest.astype(jnp.bfloat16)
        low = (rest - middle.astype(jnp.float32)).astype(jnp.bfloat16)
        rows_back = result[owner_of(k)]
        return sum(
            lax.dot_general(
                part, rows_back, (((0,), (0,)), ((), ())), preferred_element_type=jnp.float32
            )
            for part in (low, middle, high)
        )

    for k in range(1, owners):
        back_send[k] = combine(k)
        send(
            back_send.at[k], back_recv.at[exp], b_ssem.at[k], b_rsem.at[exp], (ctx, owner_of(k))
        )
    answer = combine(0)
    for k in range(1, owners):
        owner = owner_of(k)
        arrived(back_recv.at[owner], b_rsem.at[owner])
        answer = answer + back_recv[owner]
    out_ref[...] = answer.astype(out_ref.dtype)
    for copy in sent:
        copy.wait_send()


def experts(moe_input, routes, gate_values, w_gate, w_up, w_down):
    n, owners = lax.axis_size("ctx"), lax.axis_size("exp")
    held, depth, ff = w_gate.shape
    count, local_width = moe_input.shape
    pad = ((0, 8 - TOPK), (0, 128 - count))
    table = jnp.concatenate(
        [jnp.pad(routes.T.astype(jnp.float32), pad), jnp.pad(gate_values.T, pad)], axis=0
    )
    half = owners * CAP // 2
    pairs = held // 2
    nz = n // 4
    subs = nz // pairs
    width = ff * (half // 16) // subs
    dma = pltpu.SemaphoreType.DMA
    bf16, f32 = jnp.bfloat16, jnp.float32
    vm = pltpu.VMEM
    scratch = [
        vm((held, depth, ff), bf16), vm((held, depth, ff), bf16), vm((held, ff, depth), bf16),
        dma((3, pairs, 2)),
        vm((owners, 16, 128), f32), vm((owners, count, local_width), bf16),
        dma((2, owners)), dma((2, owners)),
        vm((held, owners * CAP, local_width), bf16),
        vm((pairs, 2, half, 2 * ff), f32), vm((pairs, 2, half, 2 * ff), bf16),
        vm((pairs, 2, half, 2 * ff), bf16), dma((pairs, 2)), dma((pairs, 2)),
        vm((pairs, half, 2 * ff), bf16), vm((pairs, half, 2 * ff), bf16), dma((pairs,)), dma((pairs,)),
        vm((pairs, subs, 16, 2 * width), bf16), vm((nz, 16, 2 * width), bf16),
        vm((subs, 16, 2 * width), f32), dma((pairs, subs)), dma((nz,)),
        vm((nz, 2, 2, 16, width), bf16),
        dma((nz,)), dma((nz,)), dma((nz,)), dma((nz,)), dma((2, nz)), dma((2, nz)),
        vm((owners, held * CAP, local_width), bf16),
        vm((owners, count, local_width), f32), vm((owners, count, local_width), f32),
        dma((owners,)), dma((owners,)),
    ]
    any_space = pl.BlockSpec(memory_space=pl.ANY)
    in_vmem = pl.BlockSpec(memory_space=pltpu.VMEM)
    return pl.pallas_call(
        functools.partial(expert_kernel, n, owners),
        out_shape=jax.ShapeDtypeStruct(moe_input.shape, moe_input.dtype),
        in_specs=[in_vmem, in_vmem, any_space, any_space, any_space],
        out_specs=in_vmem,
        scratch_shapes=scratch,
        compiler_params=pltpu.CompilerParams(
            collective_id=0, has_side_effects=True, vmem_limit_bytes=56 * 2**20
        ),
        cost_estimate=pl.CostEstimate(
            flops=6 * held * owners * CAP * depth * ff,
            bytes_accessed=3 * held * depth * ff * 2,
            transcendentals=0,
        ),
        name="experts",
    )(table, moe_input, w_gate, w_up, w_down)


def local(queries, latents, offsets, moe_input, routes, gate_values, w_gate, w_up, w_down):
    every_key = lax.all_gather(latents, "ctx", axis=0, tiled=True)
    moe_output = experts(moe_input, routes, gate_values, w_gate, w_up, w_down)
    attention_out = attend(queries, every_key, offsets)
    return (attention_out, moe_output)


def solution(mesh):
    return jax.shard_map(
        local,
        mesh=mesh,
        in_specs=(
            P(("ctx", "exp"), None),
            P("ctx", None),
            P(("ctx", "exp")),
            P("exp", "ctx"),
            P("exp", None),
            P("exp", None),
            P("exp", "ctx", None),
            P("exp", "ctx", None),
            P("exp", None, "ctx"),
        ),
        out_specs=(P(("ctx", "exp"), None), P("exp", "ctx")),
        check_vma=False,
    )
```

```python
import functools

import jax
import jax.numpy as jnp
from jax import lax
from jax.experimental import pallas as pl
from jax.experimental.pallas import tpu as pltpu
from jax.sharding import PartitionSpec as P

H = 128
LAT = 512
ROPE = 64
TOPK = 6
EXPERTS = 16
CAP = 16
MESH = pl.DeviceIdType.MESH

softmax_scale = 192.0 ** (-0.5)


def expert_kernel(
    n, owners,
    offset_ref, query_ref, latent_ref, table_ref, tokens_ref, gate_hbm, up_hbm, down_hbm,
    attention_ref, out_ref,
    keys, kz_ssem, kz_rsem, kx_ssem, kx_rsem, kc_ssem, kc_rsem, ordered, mixture,
    gate_w, up_w, down_w, w_sem,
    tables, tokens, t_ssem, t_rsem, x_rows,
    keep, core_send, core_recv, c_ssem, c_rsem,
    side_send, side_recv, s_ssem, s_rsem,
    far_send, far_recv, own, f_ssem, f_rsem,
    hidden, hz_ssem, hz_rsem, hx_ssem, hx_rsem, hc_ssem, hc_rsem,
    result, back_send, back_recv, b_ssem, b_rsem,
):
    held = gate_hbm.shape[0]
    ff = gate_hbm.shape[2]
    count = tokens_ref.shape[0]
    rows = owners * CAP
    half = rows // 2
    pairs = held // 2
    nz = n // 4
    subs = nz // pairs
    block_rows = latent_ref.shape[0]
    query_count = query_ref.shape[0]
    row_blocks = half // 16
    col_blocks = subs // row_blocks
    width = ff // col_blocks

    ctx = lax.axis_index("ctx")
    exp = lax.axis_index("exp")
    core = lax.rem(ctx, 2)
    side = lax.rem(ctx // 2, 2)
    far = ctx // 4
    sibling = (ctx + 1 - 2 * core, exp)
    beside = (ctx + 2 - 4 * side, exp)

    def at_far(index):
        return (index * 4 + side * 2 + core, exp)

    def far_of(step):
        return lax.rem(far + step, nz)

    def owner_of(step):
        return lax.rem(exp + step, owners)

    pair_of = [lax.rem(far // subs + 1 + i, pairs) for i in range(pairs)]
    weight_copies = {}
    for i in range(pairs):
        for j in range(2):
            expert = pair_of[i] * 2 + (1 - side if j == 0 else side)
            weight_copies[i, j] = [
                pltpu.make_async_copy(hbm.at[expert], vmem.at[expert], w_sem.at[k, i, j])
                for k, (hbm, vmem) in enumerate(((gate_hbm, gate_w), (up_hbm, up_w)))
            ]
            for copy in weight_copies[i, j]:
                copy.start()
    down_order = [(d, j) for d in range(pairs) for j in range(2)]
    down_expert = {}
    down_copies = {}
    for d, j in down_order:
        expert = lax.rem(far // subs + d, pairs) * 2 + (side if j == 0 else 1 - side)
        down_expert[d, j] = expert
        down_copies[d, j] = pltpu.make_async_copy(
            down_hbm.at[expert], down_w.at[expert], w_sem.at[2, d, j]
        )
        down_copies[d, j].start()

    barrier = pltpu.get_barrier_semaphore()
    greeted = [sibling, beside]
    greeted += [at_far(far_of(k)) for k in range(1, nz)]
    greeted += [(ctx, owner_of(k)) for k in range(1, owners)]
    for device in greeted:
        pl.semaphore_signal(barrier, inc=1, device_id=device, device_id_type=MESH)
    pl.semaphore_wait(barrier, len(greeted))

    sent = []

    def send(src, dst, ssem, rsem, device):
        copy = pltpu.make_async_remote_copy(
            src_ref=src, dst_ref=dst, send_sem=ssem, recv_sem=rsem,
            device_id=device, device_id_type=MESH,
        )
        copy.start()
        sent.append(copy)

    def arrived(dst, sem):
        pltpu.make_async_remote_copy(
            src_ref=dst, dst_ref=dst, send_sem=sem, recv_sem=sem,
            device_id=sibling, device_id_type=MESH,
        ).wait_recv()

    for k in range(1, owners):
        device = (ctx, owner_of(k))
        send(table_ref, tables.at[exp], t_ssem.at[0, k], t_rsem.at[0, exp], device)
        send(tokens_ref, tokens.at[exp], t_ssem.at[1, k], t_rsem.at[1, exp], device)

    def keys_at(where, slot_side, slot_core):
        start = (where * 4 + slot_side * 2 + slot_core) * block_rows
        return keys.at[pl.ds(pl.multiple_of(start, 16), block_rows)]

    own_keys = keys_at(far, side, core)
    own_keys[...] = latent_ref[...]
    for k in range(1, nz):
        send(own_keys, own_keys, kz_ssem.at[k], kz_rsem.at[far], at_far(far_of(k)))

    def keys_here(k):
        where = far_of(nz - k) if k else far
        here = keys_at(where, side, core)
        if k:
            arrived(here, kz_rsem.at[where])
        send(here, here, kx_ssem.at[k], kx_rsem.at[where], beside)
        send(here, here, kc_ssem.at[0, k], kc_rsem.at[0, where], sibling)

    def keys_beside(k):
        where = far_of(nz - k) if k else far
        here = keys_at(where, 1 - side, core)
        arrived(here, kx_rsem.at[where])
        send(here, here, kc_ssem.at[1, k], kc_rsem.at[1, where], sibling)

    def keys_complete():
        for where in range(nz):
            for j in range(2):
                slot_side = side if j == 0 else 1 - side
                arrived(keys_at(where, slot_side, 1 - core), kc_rsem.at[j, where])

    keys_here(0)

    wide = 2 * (LAT + ROPE)
    pair_rows = 2 * query_count

    @pl.loop(0, H // 2)
    def _(at):
        two = query_ref[:, pl.ds(pl.multiple_of(at * wide, 128), wide)].astype(jnp.float32)
        ordered[pl.ds(pl.multiple_of(at * pair_rows, 8), pair_rows), :] = jnp.concatenate(
            [two[:, : LAT + ROPE], two[:, LAT + ROPE :]], axis=0
        )

    def attend(chunk):
        height = mixture.shape[0]
        scores = (
            lax.dot_general(
                ordered[chunk * height : (chunk + 1) * height, :].astype(jnp.bfloat16),
                keys[...],
                (((1,), (1,)), ((), ())),
                preferred_element_type=jnp.float32,
            )
            * softmax_scale
        )
        key_pos = lax.broadcasted_iota(jnp.int32, scores.shape, 1)
        query_pos = offset_ref[0] + lax.rem(
            lax.broadcasted_iota(jnp.int32, (height, 1), 0), query_count
        )
        scores = jnp.where(key_pos <= query_pos, scores, -jnp.inf)
        weights = jnp.exp(scores - jnp.max(scores, axis=1, keepdims=True))
        denominator = jnp.sum(weights, axis=1, keepdims=True)
        mixed = jnp.dot(
            weights.astype(jnp.bfloat16), keys[:, :LAT], preferred_element_type=jnp.float32
        )
        mixture[...] = mixed / denominator

        @pl.loop(0, height // pair_rows)
        def _(at):
            two = mixture[pl.ds(pl.multiple_of(at * pair_rows, 8), pair_rows), :]
            start = (chunk * (height // pair_rows) + at) * 2 * LAT
            for k in range(2):
                attention_ref[:, pl.ds(pl.multiple_of(start + k * LAT, 128), LAT)] = two[
                    k * query_count : (k + 1) * query_count
                ].astype(attention_ref.dtype)

    first = exp * held
    expert_ids = (lax.broadcasted_iota(jnp.int32, (held, count), 0) + first).astype(jnp.float32)
    earlier = (
        lax.broadcasted_iota(jnp.int32, (count, count), 0)
        < lax.broadcasted_iota(jnp.int32, (count, count), 1)
    ).astype(jnp.bfloat16)
    slots = lax.broadcasted_iota(jnp.int32, (held, CAP, count), 1).astype(jnp.float32)

    def placement(table):
        named = jnp.zeros((held, count), jnp.float32)
        gates = jnp.zeros((held, count), jnp.float32)
        for k in range(TOPK):
            hit = table[k : k + 1, :count] == expert_ids
            named = jnp.where(hit, 1.0, named)
            gates = jnp.where(hit, table[8 + k : 9 + k, :count], gates)
        rank = jnp.dot(named.astype(jnp.bfloat16), earlier, preferred_element_type=jnp.float32)
        rank = jnp.where(named > 0.5, rank, -1.0)
        picked = rank[:, None, :] == slots
        chosen = jnp.where(picked, 1.0, 0.0).reshape(held * CAP, count)
        weighted = jnp.where(picked, gates[:, None, :], 0.0).reshape(held * CAP, count)
        return chosen.astype(jnp.bfloat16), weighted

    def place(table, values, owner):
        chosen, weighted = placement(table)
        placed = jnp.dot(chosen, values, preferred_element_type=jnp.float32).astype(jnp.bfloat16)
        for e in range(held):
            x_rows[e, pl.ds(pl.multiple_of(owner * CAP, CAP), CAP), :] = placed[e * CAP : (e + 1) * CAP]
        return weighted

    weighted_of = {0: place(table_ref[...], tokens_ref[...], exp)}
    for k in range(1, owners):
        owner = owner_of(k)
        arrived(tables.at[owner], t_rsem.at[0, owner])
        arrived(tokens.at[owner], t_rsem.at[1, owner])
        weighted_of[k] = place(tables[owner], tokens[owner], owner)

    mine = pl.ds(pl.multiple_of(core * half, 16), half)
    other = pl.ds(pl.multiple_of((1 - core) * half, 16), half)

    def multiply(i):
        for j in range(2):
            expert = pair_of[i] * 2 + (1 - side if j == 0 else side)
            for k, weight in ((0, gate_w), (1, up_w)):
                weight_copies[i, j][k].wait()
                columns = slice(k * ff, (k + 1) * ff)
                keep[i, j, :, columns] = jnp.dot(
                    x_rows[expert], weight[expert], preferred_element_type=jnp.float32
                )
            core_send[i, j] = keep[i, j, other, :].astype(jnp.bfloat16)
            send(core_send.at[i, j], core_recv.at[i, j], c_ssem.at[i, j], c_rsem.at[i, j], sibling)

    def to_side(i):
        arrived(core_recv.at[i, 0], c_rsem.at[i, 0])
        side_send[i] = (keep[i, 0, mine, :] + core_recv[i, 0].astype(jnp.float32)).astype(jnp.bfloat16)
        send(side_send.at[i], side_recv.at[i], s_ssem.at[i], s_rsem.at[i], beside)

    def block(i, sub):
        row = lax.rem(sub, row_blocks)
        return i, row, sub // row_blocks

    def to_far(i):
        arrived(core_recv.at[i, 1], c_rsem.at[i, 1])
        arrived(side_recv.at[i], s_rsem.at[i])
        total = (
            keep[i, 1, mine, :] + core_recv[i, 1].astype(jnp.float32) + side_recv[i].astype(jnp.float32)
        )
        for r in range(row_blocks):
            for c in range(col_blocks):
                for k in range(2):
                    piece = total[r * 16 : r * 16 + 16, k * ff + c * width : k * ff + (c + 1) * width]
                    at = c * row_blocks + r
                    far_send[i, at, :, k * width : (k + 1) * width] = piece.astype(jnp.bfloat16)
                    if i == pairs - 1:
                        own[at, :, k * width : (k + 1) * width] = piece
        my_sub = lax.rem(far, subs)
        for s in range(subs if i < pairs - 1 else subs - 1):
            sub = lax.rem(my_sub + 1 + s, subs)
            dest = pair_of[i] * subs + sub
            send(
                far_send.at[i, sub], far_recv.at[far], f_ssem.at[i, s], f_rsem.at[far], at_far(dest)
            )

    forwards = [functools.partial(keys_here, k) for k in range(1, nz)]
    forwards += [functools.partial(keys_beside, k) for k in range(nz)]
    chunks = ordered.shape[0] // mixture.shape[0]
    share = -(-len(forwards) // max(pairs - 1, 1))
    for t in range(pairs + 2):
        if t < pairs:
            multiply(t)
        if t == pairs:
            keys_complete()
            attend(0)
        if t == pairs + 1:
            attend(1)
        if 0 <= t - 1 < pairs:
            to_side(t - 1)
        if 0 <= t - 2 < pairs:
            to_far(t - 2)
        if t < pairs:
            for forward in forwards[max(t - 1, 0) * share : t * share] if pairs > 1 else forwards:
                forward()
    for chunk in range(2, chunks):
        attend(chunk)

    total = own[lax.rem(far, subs)]
    for k in range(1, nz):
        sender = far_of(nz - k)
        arrived(far_recv.at[sender], f_rsem.at[sender])
        total = total + far_recv[sender].astype(jnp.float32)
    gate, up = total[:, :width], total[:, width:]
    hidden[far, side, core] = (gate / (1.0 + jnp.exp(-gate)) * up).astype(jnp.bfloat16)

    def pass_on(where, slot_side, ssems, rsems, device):
        here = hidden.at[where, slot_side, core]
        send(here, here, ssems, rsems, device)

    mine_block = hidden.at[far, side, core]
    for k in range(1, nz):
        send(mine_block, mine_block, hz_ssem.at[k], hz_rsem.at[far], at_far(far_of(k)))
    for k in range(nz):
        where = far_of(nz - k) if k else far
        if k:
            arrived(hidden.at[where, side, core], hz_rsem.at[where])
        pass_on(where, side, hx_ssem.at[k], hx_rsem.at[where], beside)
        pass_on(where, side, hc_ssem.at[0, k], hc_rsem.at[0, where], sibling)
    for k in range(nz):
        where = far_of(nz - k) if k else far
        arrived(hidden.at[where, 1 - side, core], hx_rsem.at[where])
        pass_on(where, 1 - side, hc_ssem.at[1, k], hc_rsem.at[1, where], sibling)

    for j in range(2):
        slot_side = side if j == 0 else 1 - side
        for d in range(pairs):
            expert = down_expert[d, j]
            pair = lax.rem(far // subs + d, pairs)
            for s in range(subs):
                where = pair * subs + s
                arrived(hidden.at[where, slot_side, 1 - core], hc_rsem.at[j, where])
            strips = []
            for c in range(2):
                for r in range(row_blocks):
                    strips.append(
                        jnp.concatenate(
                            [
                                hidden[pair * subs + q * row_blocks + r, slot_side, c]
                                for q in range(col_blocks)
                            ],
                            axis=1,
                        )
                    )
            down_copies[d, j].wait()
            made = lax.dot_general(
                jnp.concatenate(strips, axis=0),
                down_w[expert],
                (((1,), (1,)), ((), ())),
                preferred_element_type=jnp.float32,
            ).astype(jnp.bfloat16)
            for s in range(owners):
                result[s, pl.ds(pl.multiple_of(expert * CAP, CAP), CAP), :] = made[
                    s * CAP : (s + 1) * CAP
                ]

    def combine(k):
        weighted = weighted_of[k]
        high = weighted.astype(jnp.bfloat16)
        rest = weighted - high.astype(jnp.float32)
        middle = rest.astype(jnp.bfloat16)
        low = (rest - middle.astype(jnp.float32)).astype(jnp.bfloat16)
        rows_back = result[owner_of(k)]
        return sum(
            lax.dot_general(
                part, rows_back, (((0,), (0,)), ((), ())), preferred_element_type=jnp.float32
            )
            for part in (low, middle, high)
        )

    for k in range(1, owners):
        back_send[k] = combine(k)
        send(
            back_send.at[k], back_recv.at[exp], b_ssem.at[k], b_rsem.at[exp], (ctx, owner_of(k))
        )
    answer = combine(0)
    for k in range(1, owners):
        owner = owner_of(k)
        arrived(back_recv.at[owner], b_rsem.at[owner])
        answer = answer + back_recv[owner]
    out_ref[...] = answer.astype(out_ref.dtype)
    for copy in sent:
        copy.wait_send()


def layer(queries, latents, offsets, moe_input, routes, gate_values, w_gate, w_up, w_down):
    n, owners = lax.axis_size("ctx"), lax.axis_size("exp")
    held, depth, ff = w_gate.shape
    count, local_width = moe_input.shape
    pad = ((0, 8 - TOPK), (0, 128 - count))
    table = jnp.concatenate(
        [jnp.pad(routes.T.astype(jnp.float32), pad), jnp.pad(gate_values.T, pad)], axis=0
    )
    half = owners * CAP // 2
    pairs = held // 2
    nz = n // 4
    subs = nz // pairs
    width = ff * (half // 16) // subs
    dma = pltpu.SemaphoreType.DMA
    bf16, f32 = jnp.bfloat16, jnp.float32
    vm = pltpu.VMEM
    scratch = [
        vm((n * latents.shape[0], LAT + ROPE), bf16),
        dma((nz,)), dma((nz,)), dma((nz,)), dma((nz,)), dma((2, nz)), dma((2, nz)),
        vm((queries.shape[0] * H, LAT + ROPE), f32), vm((128, LAT), f32),
        vm((held, depth, ff), bf16), vm((held, depth, ff), bf16), vm((held, depth, ff), bf16),
        dma((3, pairs, 2)),
        vm((owners, 16, 128), f32), vm((owners, count, local_width), bf16),
        dma((2, owners)), dma((2, owners)),
        vm((held, owners * CAP, local_width), bf16),
        vm((pairs, 2, 2 * half, 2 * ff), f32), vm((pairs, 2, half, 2 * ff), bf16),
        vm((pairs, 2, half, 2 * ff), bf16), dma((pairs, 2)), dma((pairs, 2)),
        vm((pairs, half, 2 * ff), bf16), vm((pairs, half, 2 * ff), bf16), dma((pairs,)), dma((pairs,)),
        vm((pairs, subs, 16, 2 * width), bf16), vm((nz, 16, 2 * width), bf16),
        vm((subs, 16, 2 * width), f32), dma((pairs, subs)), dma((nz,)),
        vm((nz, 2, 2, 16, width), bf16),
        dma((nz,)), dma((nz,)), dma((nz,)), dma((nz,)), dma((2, nz)), dma((2, nz)),
        vm((owners, held * CAP, local_width), bf16),
        vm((owners, count, local_width), f32), vm((owners, count, local_width), f32),
        dma((owners,)), dma((owners,)),
    ]
    any_space = pl.BlockSpec(memory_space=pl.ANY)
    in_vmem = pl.BlockSpec(memory_space=pltpu.VMEM)
    return pl.pallas_call(
        functools.partial(expert_kernel, n, owners),
        out_shape=[
            jax.ShapeDtypeStruct((queries.shape[0], H * LAT), bf16),
            jax.ShapeDtypeStruct(moe_input.shape, bf16),
        ],
        in_specs=[
            pl.BlockSpec(memory_space=pltpu.SMEM), in_vmem, in_vmem, in_vmem, in_vmem,
            any_space, any_space, any_space,
        ],
        out_specs=[in_vmem, in_vmem],
        scratch_shapes=scratch,
        compiler_params=pltpu.CompilerParams(
            collective_id=0, has_side_effects=True, vmem_limit_bytes=56 * 2**20
        ),
        cost_estimate=pl.CostEstimate(
            flops=6 * held * owners * CAP * depth * ff,
            bytes_accessed=3 * held * depth * ff * 2,
            transcendentals=0,
        ),
        name="layer",
    )(offsets, queries, latents, table, moe_input, w_gate, w_up, jnp.swapaxes(w_down, 1, 2))


def solution(mesh):
    return jax.shard_map(
        lambda *operands: tuple(layer(*operands)),
        mesh=mesh,
        in_specs=(
            P(("ctx", "exp"), None),
            P("ctx", None),
            P(("ctx", "exp")),
            P("exp", "ctx"),
            P("exp", None),
            P("exp", None),
            P("exp", "ctx", None),
            P("exp", "ctx", None),
            P("exp", None, "ctx"),
        ),
        out_specs=(P(("ctx", "exp"), None), P("exp", "ctx")),
        check_vma=False,
    )
```

```python
import functools

import jax
import jax.numpy as jnp
from jax import lax
from jax.experimental import pallas as pl
from jax.experimental.pallas import tpu as pltpu
from jax.sharding import PartitionSpec as P

H = 128
LAT = 512
ROPE = 64
TOPK = 6
EXPERTS = 16
CAP = 16
MESH = pl.DeviceIdType.MESH

softmax_scale = 192.0 ** (-0.5)


def expert_kernel(
    n, owners,
    offset_ref, query_ref, latent_ref, routes_ref, gates_ref, tokens_ref, gate_hbm, up_hbm, down_hbm,
    attention_ref, out_ref,
    table, keys, kz_ssem, kz_rsem, kx_ssem, kx_rsem, kc_ssem, kc_rsem, ordered, mixture,
    gate_w, up_w, down_w, w_sem,
    tables, tokens, t_ssem, t_rsem, x_rows,
    keep, core_send, core_recv, c_ssem, c_rsem,
    side_send, side_recv, s_ssem, s_rsem,
    far_send, far_recv, own, f_ssem, f_rsem,
    hidden, hz_ssem, hz_rsem, hx_ssem, hx_rsem, hc_ssem, hc_rsem,
    result, back_send, back_recv, b_ssem, b_rsem,
):
    held = gate_hbm.shape[0]
    ff = gate_hbm.shape[2]
    count = tokens_ref.shape[0]
    rows = owners * CAP
    half = rows // 2
    pairs = held // 2
    nz = n // 4
    subs = nz // pairs
    block_rows = latent_ref.shape[0]
    query_count = query_ref.shape[0]
    row_blocks = half // 16
    col_blocks = subs // row_blocks
    width = ff // col_blocks

    ctx = lax.axis_index("ctx")
    exp = lax.axis_index("exp")
    core = lax.rem(ctx, 2)
    side = lax.rem(ctx // 2, 2)
    far = ctx // 4
    sibling = (ctx + 1 - 2 * core, exp)
    beside = (ctx + 2 - 4 * side, exp)

    def at_far(index):
        return (index * 4 + side * 2 + core, exp)

    def far_of(step):
        return lax.rem(far + step, nz)

    def owner_of(step):
        return lax.rem(exp + step, owners)

    pair_of = [lax.rem(far // subs + 1 + i, pairs) for i in range(pairs)]
    weight_copies = {}
    for i in range(pairs):
        for j in range(2):
            expert = pair_of[i] * 2 + (1 - side if j == 0 else side)
            weight_copies[i, j] = [
                pltpu.make_async_copy(hbm.at[expert], vmem.at[expert], w_sem.at[k, i, j])
                for k, (hbm, vmem) in enumerate(((gate_hbm, gate_w), (up_hbm, up_w)))
            ]
    down_order = [(d, j) for d in range(pairs) for j in range(2)]
    down_expert = {}
    down_copies = {}
    for d, j in down_order:
        expert = lax.rem(far // subs + d, pairs) * 2 + (side if j == 0 else 1 - side)
        down_expert[d, j] = expert
        down_copies[d, j] = pltpu.make_async_copy(
            down_hbm.at[expert], down_w.at[expert], w_sem.at[2, d, j]
        )

    def start_weights(i):
        for j in range(2):
            for copy in weight_copies[i, j]:
                copy.start()

    for i in range(min(2, pairs)):
        start_weights(i)

    table[...] = jnp.zeros_like(table)
    table[:TOPK, :count] = routes_ref[...].astype(jnp.float32)
    table[8 : 8 + TOPK, :count] = gates_ref[...]

    barrier = pltpu.get_barrier_semaphore()
    greeted = [sibling, beside]
    greeted += [at_far(far_of(k)) for k in range(1, nz)]
    greeted += [(ctx, owner_of(k)) for k in range(1, owners)]
    for device in greeted:
        pl.semaphore_signal(barrier, inc=1, device_id=device, device_id_type=MESH)
    pl.semaphore_wait(barrier, len(greeted))

    sent = []

    def send(src, dst, ssem, rsem, device):
        copy = pltpu.make_async_remote_copy(
            src_ref=src, dst_ref=dst, send_sem=ssem, recv_sem=rsem,
            device_id=device, device_id_type=MESH,
        )
        copy.start()
        sent.append(copy)

    def arrived(dst, sem):
        pltpu.make_async_remote_copy(
            src_ref=dst, dst_ref=dst, send_sem=sem, recv_sem=sem,
            device_id=sibling, device_id_type=MESH,
        ).wait_recv()

    for k in range(1, owners):
        device = (ctx, owner_of(k))
        send(table, tables.at[exp], t_ssem.at[0, k], t_rsem.at[0, exp], device)
        send(tokens_ref, tokens.at[exp], t_ssem.at[1, k], t_rsem.at[1, exp], device)

    def keys_at(where, slot_side, slot_core):
        start = (where * 4 + slot_side * 2 + slot_core) * block_rows
        return keys.at[pl.ds(pl.multiple_of(start, 16), block_rows)]

    own_keys = keys_at(far, side, core)
    own_keys[...] = latent_ref[...]
    for k in range(1, nz):
        send(own_keys, own_keys, kz_ssem.at[k], kz_rsem.at[far], at_far(far_of(k)))

    def keys_here(k):
        where = far_of(nz - k) if k else far
        here = keys_at(where, side, core)
        if k:
            arrived(here, kz_rsem.at[where])
        send(here, here, kx_ssem.at[k], kx_rsem.at[where], beside)
        send(here, here, kc_ssem.at[0, k], kc_rsem.at[0, where], sibling)

    def keys_beside(k):
        where = far_of(nz - k) if k else far
        here = keys_at(where, 1 - side, core)
        arrived(here, kx_rsem.at[where])
        send(here, here, kc_ssem.at[1, k], kc_rsem.at[1, where], sibling)

    def keys_complete():
        for where in range(nz):
            for j in range(2):
                slot_side = side if j == 0 else 1 - side
                arrived(keys_at(where, slot_side, 1 - core), kc_rsem.at[j, where])

    keys_here(0)

    wide = 2 * (LAT + ROPE)
    pair_rows = 2 * query_count

    def order_queries():
        @pl.loop(0, H // 2, unroll=4)
        def _(at):
            two = query_ref[:, pl.ds(pl.multiple_of(at * wide, 128), wide)].astype(jnp.float32)
            ordered[pl.ds(pl.multiple_of(at * pair_rows, 8), pair_rows), :] = jnp.concatenate(
                [two[:, : LAT + ROPE], two[:, LAT + ROPE :]], axis=0
            )

    def attend(chunk):
        height = mixture.shape[0]
        scores = (
            lax.dot_general(
                ordered[chunk * height : (chunk + 1) * height, :].astype(jnp.bfloat16),
                keys[...],
                (((1,), (1,)), ((), ())),
                preferred_element_type=jnp.float32,
            )
            * softmax_scale
        )
        key_pos = lax.broadcasted_iota(jnp.int32, scores.shape, 1)
        query_pos = offset_ref[0] + lax.rem(
            lax.broadcasted_iota(jnp.int32, (height, 1), 0), query_count
        )
        scores = jnp.where(key_pos <= query_pos, scores, -jnp.inf)
        weights = jnp.exp(scores - jnp.max(scores, axis=1, keepdims=True))
        denominator = jnp.sum(weights, axis=1, keepdims=True)
        mixed = jnp.dot(
            weights.astype(jnp.bfloat16), keys[:, :LAT], preferred_element_type=jnp.float32
        )
        mixture[...] = mixed / denominator

        @pl.loop(0, height // pair_rows, unroll=4)
        def _(at):
            two = mixture[pl.ds(pl.multiple_of(at * pair_rows, 8), pair_rows), :]
            start = (chunk * (height // pair_rows) + at) * 2 * LAT
            for k in range(2):
                attention_ref[:, pl.ds(pl.multiple_of(start + k * LAT, 128), LAT)] = two[
                    k * query_count : (k + 1) * query_count
                ].astype(attention_ref.dtype)

    first = exp * held
    expert_ids = (lax.broadcasted_iota(jnp.int32, (held, count), 0) + first).astype(jnp.float32)
    earlier = (
        lax.broadcasted_iota(jnp.int32, (count, count), 0)
        < lax.broadcasted_iota(jnp.int32, (count, count), 1)
    ).astype(jnp.bfloat16)
    slots = lax.broadcasted_iota(jnp.int32, (held, CAP, count), 1).astype(jnp.float32)

    def placement(listed):
        named = jnp.zeros((held, count), jnp.float32)
        gates = jnp.zeros((held, count), jnp.float32)
        for k in range(TOPK):
            hit = listed[k : k + 1, :count] == expert_ids
            named = jnp.where(hit, 1.0, named)
            gates = jnp.where(hit, listed[8 + k : 9 + k, :count], gates)
        rank = jnp.dot(named.astype(jnp.bfloat16), earlier, preferred_element_type=jnp.float32)
        rank = jnp.where(named > 0.5, rank, -1.0)
        picked = rank[:, None, :] == slots
        chosen = jnp.where(picked, 1.0, 0.0).reshape(held * CAP, count)
        weighted = jnp.where(picked, gates[:, None, :], 0.0).reshape(held * CAP, count)
        return chosen.astype(jnp.bfloat16), weighted

    def place(listed, values, owner):
        chosen, weighted = placement(listed)
        placed = jnp.dot(chosen, values, preferred_element_type=jnp.float32).astype(jnp.bfloat16)
        for e in range(held):
            x_rows[e, pl.ds(pl.multiple_of(owner * CAP, CAP), CAP), :] = placed[e * CAP : (e + 1) * CAP]
        return weighted

    weighted_of = {0: place(table[...], tokens_ref[...], exp)}
    for k in range(1, owners):
        owner = owner_of(k)
        arrived(tables.at[owner], t_rsem.at[0, owner])
        arrived(tokens.at[owner], t_rsem.at[1, owner])
        weighted_of[k] = place(tables[owner], tokens[owner], owner)

    mine = pl.ds(pl.multiple_of(core * half, 16), half)
    other = pl.ds(pl.multiple_of((1 - core) * half, 16), half)

    def multiply(i):
        if i + 2 < pairs:
            start_weights(i + 2)
        if i == max(pairs - 2, 0):
            for key in down_order:
                down_copies[key].start()
        for j in range(2):
            expert = pair_of[i] * 2 + (1 - side if j == 0 else side)
            for k, weight in ((0, gate_w), (1, up_w)):
                weight_copies[i, j][k].wait()
                columns = slice(k * ff, (k + 1) * ff)
                keep[i, j, :, columns] = jnp.dot(
                    x_rows[expert], weight[expert], preferred_element_type=jnp.float32
                )
            core_send[i, j] = keep[i, j, other, :].astype(jnp.bfloat16)
            send(core_send.at[i, j], core_recv.at[i, j], c_ssem.at[i, j], c_rsem.at[i, j], sibling)

    def to_side(i):
        arrived(core_recv.at[i, 0], c_rsem.at[i, 0])
        side_send[i] = (keep[i, 0, mine, :] + core_recv[i, 0].astype(jnp.float32)).astype(jnp.bfloat16)
        send(side_send.at[i], side_recv.at[i], s_ssem.at[i], s_rsem.at[i], beside)

    def block(i, sub):
        row = lax.rem(sub, row_blocks)
        return i, row, sub // row_blocks

    def to_far(i):
        arrived(core_recv.at[i, 1], c_rsem.at[i, 1])
        arrived(side_recv.at[i], s_rsem.at[i])
        total = (
            keep[i, 1, mine, :] + core_recv[i, 1].astype(jnp.float32) + side_recv[i].astype(jnp.float32)
        )
        for r in range(row_blocks):
            for c in range(col_blocks):
                for k in range(2):
                    piece = total[r * 16 : r * 16 + 16, k * ff + c * width : k * ff + (c + 1) * width]
                    at = c * row_blocks + r
                    far_send[i, at, :, k * width : (k + 1) * width] = piece.astype(jnp.bfloat16)
                    if i == pairs - 1:
                        own[at, :, k * width : (k + 1) * width] = piece
        my_sub = lax.rem(far, subs)
        for s in range(subs if i < pairs - 1 else subs - 1):
            sub = lax.rem(my_sub + 1 + s, subs)
            dest = pair_of[i] * subs + sub
            send(
                far_send.at[i, sub], far_recv.at[far], f_ssem.at[i, s], f_rsem.at[far], at_far(dest)
            )

    forwards = [functools.partial(keys_here, k) for k in range(1, nz)]
    forwards += [functools.partial(keys_beside, k) for k in range(nz)]
    chunks = ordered.shape[0] // mixture.shape[0]
    share = -(-len(forwards) // max(pairs - 1, 1))
    for t in range(pairs):
        multiply(t)
        if t:
            to_side(t - 1)
        for forward in forwards[max(t - 1, 0) * share : t * share] if pairs > 1 else forwards:
            forward()
    to_side(pairs - 1)
    to_far(0)
    order_queries()
    for t in range(1, pairs - 1):
        to_far(t)
    keys_complete()
    for chunk in range(chunks):
        attend(chunk)
        if chunk == 0 and pairs > 1:
            to_far(pairs - 1)

    total = own[lax.rem(far, subs)]
    for k in range(1, nz):
        sender = far_of(nz - k)
        arrived(far_recv.at[sender], f_rsem.at[sender])
        total = total + far_recv[sender].astype(jnp.float32)
    gate, up = total[:, :width], total[:, width:]
    hidden[far, side, core] = (gate / (1.0 + jnp.exp(-gate)) * up).astype(jnp.bfloat16)

    def pass_on(where, slot_side, ssems, rsems, device):
        here = hidden.at[where, slot_side, core]
        send(here, here, ssems, rsems, device)

    mine_block = hidden.at[far, side, core]
    for k in range(1, nz):
        send(mine_block, mine_block, hz_ssem.at[k], hz_rsem.at[far], at_far(far_of(k)))
    for k in range(nz):
        where = far_of(nz - k) if k else far
        if k:
            arrived(hidden.at[where, side, core], hz_rsem.at[where])
        pass_on(where, side, hx_ssem.at[k], hx_rsem.at[where], beside)
        pass_on(where, side, hc_ssem.at[0, k], hc_rsem.at[0, where], sibling)
    for k in range(nz):
        where = far_of(nz - k) if k else far
        arrived(hidden.at[where, 1 - side, core], hx_rsem.at[where])
        pass_on(where, 1 - side, hc_ssem.at[1, k], hc_rsem.at[1, where], sibling)

    for j in range(2):
        slot_side = side if j == 0 else 1 - side
        for d in range(pairs):
            expert = down_expert[d, j]
            pair = lax.rem(far // subs + d, pairs)
            for s in range(subs):
                where = pair * subs + s
                arrived(hidden.at[where, slot_side, 1 - core], hc_rsem.at[j, where])
            strips = []
            for c in range(2):
                for r in range(row_blocks):
                    strips.append(
                        jnp.concatenate(
                            [
                                hidden[pair * subs + q * row_blocks + r, slot_side, c]
                                for q in range(col_blocks)
                            ],
                            axis=1,
                        )
                    )
            down_copies[d, j].wait()
            made = lax.dot_general(
                jnp.concatenate(strips, axis=0),
                down_w[expert],
                (((1,), (1,)), ((), ())),
                preferred_element_type=jnp.float32,
            ).astype(jnp.bfloat16)
            for s in range(owners):
                result[s, pl.ds(pl.multiple_of(expert * CAP, CAP), CAP), :] = made[
                    s * CAP : (s + 1) * CAP
                ]

    def combine(k):
        weighted = weighted_of[k]
        high = weighted.astype(jnp.bfloat16)
        rest = weighted - high.astype(jnp.float32)
        middle = rest.astype(jnp.bfloat16)
        low = (rest - middle.astype(jnp.float32)).astype(jnp.bfloat16)
        rows_back = result[owner_of(k)]
        return sum(
            lax.dot_general(
                part, rows_back, (((0,), (0,)), ((), ())), preferred_element_type=jnp.float32
            )
            for part in (low, middle, high)
        )

    for k in range(1, owners):
        back_send[k] = combine(k)
        send(
            back_send.at[k], back_recv.at[exp], b_ssem.at[k], b_rsem.at[exp], (ctx, owner_of(k))
        )
    answer = combine(0)
    for k in range(1, owners):
        owner = owner_of(k)
        arrived(back_recv.at[owner], b_rsem.at[owner])
        answer = answer + back_recv[owner]
    out_ref[...] = answer.astype(out_ref.dtype)
    for copy in sent:
        copy.wait_send()


def layer(queries, latents, offsets, moe_input, routes, gate_values, w_gate, w_up, w_down):
    n, owners = lax.axis_size("ctx"), lax.axis_size("exp")
    held, depth, ff = w_gate.shape
    count, local_width = moe_input.shape
    half = owners * CAP // 2
    pairs = held // 2
    nz = n // 4
    subs = nz // pairs
    width = ff * (half // 16) // subs
    dma = pltpu.SemaphoreType.DMA
    bf16, f32 = jnp.bfloat16, jnp.float32
    vm = pltpu.VMEM
    scratch = [
        vm((16, 128), f32), vm((n * latents.shape[0], LAT + ROPE), bf16),
        dma((nz,)), dma((nz,)), dma((nz,)), dma((nz,)), dma((2, nz)), dma((2, nz)),
        vm((queries.shape[0] * H, LAT + ROPE), f32), vm((128, LAT), f32),
        vm((held, depth, ff), bf16), vm((held, depth, ff), bf16), vm((held, depth, ff), bf16),
        dma((3, pairs, 2)),
        vm((owners, 16, 128), f32), vm((owners, count, local_width), bf16),
        dma((2, owners)), dma((2, owners)),
        vm((held, owners * CAP, local_width), bf16),
        vm((pairs, 2, 2 * half, 2 * ff), f32), vm((pairs, 2, half, 2 * ff), bf16),
        vm((pairs, 2, half, 2 * ff), bf16), dma((pairs, 2)), dma((pairs, 2)),
        vm((pairs, half, 2 * ff), bf16), vm((pairs, half, 2 * ff), bf16), dma((pairs,)), dma((pairs,)),
        vm((pairs, subs, 16, 2 * width), bf16), vm((nz, 16, 2 * width), bf16),
        vm((subs, 16, 2 * width), f32), dma((pairs, subs)), dma((nz,)),
        vm((nz, 2, 2, 16, width), bf16),
        dma((nz,)), dma((nz,)), dma((nz,)), dma((nz,)), dma((2, nz)), dma((2, nz)),
        vm((owners, held * CAP, local_width), bf16),
        vm((owners, count, local_width), f32), vm((owners, count, local_width), f32),
        dma((owners,)), dma((owners,)),
    ]
    any_space = pl.BlockSpec(memory_space=pl.ANY)
    in_vmem = pl.BlockSpec(memory_space=pltpu.VMEM)
    return pl.pallas_call(
        functools.partial(expert_kernel, n, owners),
        out_shape=[
            jax.ShapeDtypeStruct((queries.shape[0], H * LAT), bf16),
            jax.ShapeDtypeStruct(moe_input.shape, bf16),
        ],
        in_specs=[
            pl.BlockSpec(memory_space=pltpu.SMEM), in_vmem, in_vmem, in_vmem, in_vmem, in_vmem,
            any_space, any_space, any_space,
        ],
        out_specs=[in_vmem, in_vmem],
        scratch_shapes=scratch,
        compiler_params=pltpu.CompilerParams(
            collective_id=0, has_side_effects=True, vmem_limit_bytes=56 * 2**20
        ),
        cost_estimate=pl.CostEstimate(
            flops=6 * held * owners * CAP * depth * ff,
            bytes_accessed=3 * held * depth * ff * 2,
            transcendentals=0,
        ),
        name="layer",
    )(
        offsets, queries, latents, routes.T, gate_values.T, moe_input,
        w_gate, w_up, jnp.swapaxes(w_down, 1, 2),
    )


def solution(mesh):
    return jax.shard_map(
        lambda *operands: tuple(layer(*operands)),
        mesh=mesh,
        in_specs=(
            P(("ctx", "exp"), None),
            P("ctx", None),
            P(("ctx", "exp")),
            P("exp", "ctx"),
            P("exp", None),
            P("exp", None),
            P("exp", "ctx", None),
            P("exp", "ctx", None),
            P("exp", None, "ctx"),
        ),
        out_specs=(P(("ctx", "exp"), None), P("exp", "ctx")),
        check_vma=False,
    )
```

```python
import functools

import jax
import jax.numpy as jnp
from jax import lax
from jax.experimental import pallas as pl
from jax.experimental.pallas import tpu as pltpu
from jax.sharding import PartitionSpec as P

H = 128
LAT = 512
ROPE = 64
TOPK = 6
EXPERTS = 16
CAP = 16
MESH = pl.DeviceIdType.MESH

softmax_scale = 192.0 ** (-0.5)


def expert_kernel(
    n, owners,
    offset_ref, query_ref, latent_ref, routes_ref, gates_ref, tokens_ref, gate_hbm, up_hbm, down_hbm,
    attention_ref, out_ref,
    table, keys, kz_ssem, kz_rsem, kx_ssem, kx_rsem, kc_ssem, kc_rsem, ky_ssem, ky_rsem, ordered, mixture,
    gate_w, up_w, down_w, w_sem,
    tables, tokens, t_ssem, t_rsem, x_rows,
    keep, core_send, core_recv, c_ssem, c_rsem,
    side_send, side_recv, s_ssem, s_rsem,
    far_send, far_recv, own, f_ssem, f_rsem,
    hidden, hz_ssem, hz_rsem, hx_ssem, hx_rsem, hc_ssem, hc_rsem,
    result, back_send, back_recv, b_ssem, b_rsem,
):
    held = gate_hbm.shape[0]
    ff = gate_hbm.shape[2]
    count = tokens_ref.shape[0]
    rows = owners * CAP
    half = rows // 2
    pairs = held // 2
    nz = n // 4
    subs = nz // pairs
    block_rows = latent_ref.shape[0]
    query_count = query_ref.shape[0]
    row_blocks = half // 16
    col_blocks = subs // row_blocks
    width = ff // col_blocks

    ctx = lax.axis_index("ctx")
    exp = lax.axis_index("exp")
    core = lax.rem(ctx, 2)
    side = lax.rem(ctx // 2, 2)
    far = ctx // 4
    sibling = (ctx + 1 - 2 * core, exp)
    beside = (ctx + 2 - 4 * side, exp)

    def at_far(index):
        return (index * 4 + side * 2 + core, exp)

    def far_of(step):
        return lax.rem(far + step, nz)

    def owner_of(step):
        return lax.rem(exp + step, owners)

    pair_of = [lax.rem(far // subs + 1 + i, pairs) for i in range(pairs)]
    weight_copies = {}
    for i in range(pairs):
        for j in range(2):
            expert = pair_of[i] * 2 + (1 - side if j == 0 else side)
            weight_copies[i, j] = [
                pltpu.make_async_copy(hbm.at[expert], vmem.at[expert], w_sem.at[k, i, j])
                for k, (hbm, vmem) in enumerate(((gate_hbm, gate_w), (up_hbm, up_w)))
            ]
    down_order = [(d, j) for d in range(pairs) for j in range(2)]
    down_expert = {}
    down_copies = {}
    for d, j in down_order:
        expert = lax.rem(far // subs + d, pairs) * 2 + (side if j == 0 else 1 - side)
        down_expert[d, j] = expert
        down_copies[d, j] = pltpu.make_async_copy(
            down_hbm.at[expert], down_w.at[expert], w_sem.at[2, d, j]
        )

    def start_weights(i):
        for j in range(2):
            for copy in weight_copies[i, j]:
                copy.start()

    for i in range(min(2, pairs)):
        start_weights(i)

    table[...] = jnp.zeros_like(table)
    table[:TOPK, :count] = routes_ref[...].astype(jnp.float32)
    table[8 : 8 + TOPK, :count] = gates_ref[...]

    barrier = pltpu.get_barrier_semaphore()
    greeted = [sibling, beside]
    greeted += [at_far(far_of(k)) for k in range(1, nz)]
    greeted += [(ctx, owner_of(k)) for k in range(1, owners)]
    for device in greeted:
        pl.semaphore_signal(barrier, inc=1, device_id=device, device_id_type=MESH)
    pl.semaphore_wait(barrier, len(greeted))

    sent = []

    def send(src, dst, ssem, rsem, device):
        copy = pltpu.make_async_remote_copy(
            src_ref=src, dst_ref=dst, send_sem=ssem, recv_sem=rsem,
            device_id=device, device_id_type=MESH,
        )
        copy.start()
        sent.append(copy)

    def arrived(dst, sem):
        pltpu.make_async_remote_copy(
            src_ref=dst, dst_ref=dst, send_sem=sem, recv_sem=sem,
            device_id=sibling, device_id_type=MESH,
        ).wait_recv()

    for k in range(1, owners):
        device = (ctx, owner_of(k))
        send(table, tables.at[exp], t_ssem.at[0, k], t_rsem.at[0, exp], device)
        send(tokens_ref, tokens.at[exp], t_ssem.at[1, k], t_rsem.at[1, exp], device)

    def keys_at(where, slot_side, slot_core):
        start = (where * 4 + slot_side * 2 + slot_core) * block_rows
        return keys.at[pl.ds(pl.multiple_of(start, 16), block_rows)]

    shared = owners == 2
    active = core == exp
    across = (ctx, owner_of(1))
    sent_active = []

    def if_active(body):
        if shared:
            pl.when(active)(body)
        else:
            body()

    def remote(src, ssem, rsem, device):
        copy = pltpu.make_async_remote_copy(
            src_ref=src, dst_ref=src, send_sem=ssem, recv_sem=rsem,
            device_id=device, device_id_type=MESH,
        )
        sent_active.append(copy)
        return copy

    own_keys = keys_at(far, side, core)
    own_copies = [
        remote(own_keys, kz_ssem.at[k], kz_rsem.at[far], at_far(far_of(k))) for k in range(1, nz)
    ]

    @if_active
    def _():
        own_keys[...] = latent_ref[...]
        for copy in own_copies:
            copy.start()

    def keys_step(j, k):
        where = far_of(nz - k) if k else far
        here = keys_at(where, side if j == 0 else 1 - side, core)
        copies = []
        if j == 0:
            copies.append(remote(here, kx_ssem.at[k], kx_rsem.at[where], beside))
        if shared:
            copies.append(remote(here, ky_ssem.at[j, k], ky_rsem.at[j, where], across))

        @if_active
        def _():
            if j == 0 and k:
                arrived(here, kz_rsem.at[where])
            if j == 1:
                arrived(here, kx_rsem.at[where])
            for copy in copies:
                copy.start()

        if shared:

            @pl.when(jnp.logical_not(active))
            def _():
                arrived(here, ky_rsem.at[j, where])

        send(here, here, kc_ssem.at[j, k], kc_rsem.at[j, where], sibling)

    keys_here = functools.partial(keys_step, 0)
    keys_beside = functools.partial(keys_step, 1)

    def keys_complete():
        for where in range(nz):
            for j in range(2):
                slot_side = side if j == 0 else 1 - side
                arrived(keys_at(where, slot_side, 1 - core), kc_rsem.at[j, where])

    wide = 2 * (LAT + ROPE)
    pair_rows = 2 * query_count

    def order_queries():
        @pl.loop(0, H // 2, unroll=4)
        def _(at):
            two = query_ref[:, pl.ds(pl.multiple_of(at * wide, 128), wide)].astype(jnp.float32)
            ordered[pl.ds(pl.multiple_of(at * pair_rows, 8), pair_rows), :] = jnp.concatenate(
                [two[:, : LAT + ROPE], two[:, LAT + ROPE :]], axis=0
            )

    def attend(chunk):
        height = mixture.shape[0]
        scores = (
            lax.dot_general(
                ordered[chunk * height : (chunk + 1) * height, :].astype(jnp.bfloat16),
                keys[...],
                (((1,), (1,)), ((), ())),
                preferred_element_type=jnp.float32,
            )
            * softmax_scale
        )
        key_pos = lax.broadcasted_iota(jnp.int32, scores.shape, 1)
        query_pos = offset_ref[0] + lax.rem(
            lax.broadcasted_iota(jnp.int32, (height, 1), 0), query_count
        )
        scores = jnp.where(key_pos <= query_pos, scores, -jnp.inf)
        weights = jnp.exp(scores - jnp.max(scores, axis=1, keepdims=True))
        denominator = jnp.sum(weights, axis=1, keepdims=True)
        mixed = jnp.dot(
            weights.astype(jnp.bfloat16), keys[:, :LAT], preferred_element_type=jnp.float32
        )
        mixture[...] = mixed / denominator

        @pl.loop(0, height // pair_rows, unroll=4)
        def _(at):
            two = mixture[pl.ds(pl.multiple_of(at * pair_rows, 8), pair_rows), :]
            start = (chunk * (height // pair_rows) + at) * 2 * LAT
            for k in range(2):
                attention_ref[:, pl.ds(pl.multiple_of(start + k * LAT, 128), LAT)] = two[
                    k * query_count : (k + 1) * query_count
                ].astype(attention_ref.dtype)

    first = exp * held
    expert_ids = (lax.broadcasted_iota(jnp.int32, (held, count), 0) + first).astype(jnp.float32)
    earlier = (
        lax.broadcasted_iota(jnp.int32, (count, count), 0)
        < lax.broadcasted_iota(jnp.int32, (count, count), 1)
    ).astype(jnp.bfloat16)
    slots = lax.broadcasted_iota(jnp.int32, (held, CAP, count), 1).astype(jnp.float32)

    def placement(listed):
        named = jnp.zeros((held, count), jnp.float32)
        gates = jnp.zeros((held, count), jnp.float32)
        for k in range(TOPK):
            hit = listed[k : k + 1, :count] == expert_ids
            named = jnp.where(hit, 1.0, named)
            gates = jnp.where(hit, listed[8 + k : 9 + k, :count], gates)
        rank = jnp.dot(named.astype(jnp.bfloat16), earlier, preferred_element_type=jnp.float32)
        rank = jnp.where(named > 0.5, rank, -1.0)
        picked = rank[:, None, :] == slots
        chosen = jnp.where(picked, 1.0, 0.0).reshape(held * CAP, count)
        weighted = jnp.where(picked, gates[:, None, :], 0.0).reshape(held * CAP, count)
        return chosen.astype(jnp.bfloat16), weighted

    def place(listed, values, owner):
        chosen, weighted = placement(listed)
        placed = jnp.dot(chosen, values, preferred_element_type=jnp.float32).astype(jnp.bfloat16)
        for e in range(held):
            x_rows[e, pl.ds(pl.multiple_of(owner * CAP, CAP), CAP), :] = placed[e * CAP : (e + 1) * CAP]
        return weighted

    weighted_of = {0: place(table[...], tokens_ref[...], exp)}
    for k in range(1, owners):
        owner = owner_of(k)
        arrived(tables.at[owner], t_rsem.at[0, owner])
        arrived(tokens.at[owner], t_rsem.at[1, owner])
        weighted_of[k] = place(tables[owner], tokens[owner], owner)

    mine = pl.ds(pl.multiple_of(core * half, 16), half)
    other = pl.ds(pl.multiple_of((1 - core) * half, 16), half)

    def multiply(i):
        if i + 2 < pairs:
            start_weights(i + 2)
        if i == max(pairs - 2, 0):
            for key in down_order:
                down_copies[key].start()
        for j in range(2):
            expert = pair_of[i] * 2 + (1 - side if j == 0 else side)
            for k, weight in ((0, gate_w), (1, up_w)):
                weight_copies[i, j][k].wait()
                columns = slice(k * ff, (k + 1) * ff)
                keep[i, j, :, columns] = jnp.dot(
                    x_rows[expert], weight[expert], preferred_element_type=jnp.float32
                )
            core_send[i, j] = keep[i, j, other, :].astype(jnp.bfloat16)
            send(core_send.at[i, j], core_recv.at[i, j], c_ssem.at[i, j], c_rsem.at[i, j], sibling)

    def to_side(i):
        arrived(core_recv.at[i, 0], c_rsem.at[i, 0])
        side_send[i] = (keep[i, 0, mine, :] + core_recv[i, 0].astype(jnp.float32)).astype(jnp.bfloat16)
        send(side_send.at[i], side_recv.at[i], s_ssem.at[i], s_rsem.at[i], beside)

    def block(i, sub):
        row = lax.rem(sub, row_blocks)
        return i, row, sub // row_blocks

    def to_far(i):
        arrived(core_recv.at[i, 1], c_rsem.at[i, 1])
        arrived(side_recv.at[i], s_rsem.at[i])
        total = (
            keep[i, 1, mine, :] + core_recv[i, 1].astype(jnp.float32) + side_recv[i].astype(jnp.float32)
        )
        for r in range(row_blocks):
            for c in range(col_blocks):
                for k in range(2):
                    piece = total[r * 16 : r * 16 + 16, k * ff + c * width : k * ff + (c + 1) * width]
                    at = c * row_blocks + r
                    far_send[i, at, :, k * width : (k + 1) * width] = piece.astype(jnp.bfloat16)
                    if i == pairs - 1:
                        own[at, :, k * width : (k + 1) * width] = piece
        my_sub = lax.rem(far, subs)
        for s in range(subs if i < pairs - 1 else subs - 1):
            sub = lax.rem(my_sub + 1 + s, subs)
            dest = pair_of[i] * subs + sub
            send(
                far_send.at[i, sub], far_recv.at[far], f_ssem.at[i, s], f_rsem.at[far], at_far(dest)
            )

    forwards = [functools.partial(keys_here, k) for k in range(nz)]
    forwards += [functools.partial(keys_beside, k) for k in range(nz)]
    chunks = ordered.shape[0] // mixture.shape[0]
    share = -(-(len(forwards) - 1) // max(pairs - 1, 1))
    for t in range(pairs):
        if t == 0:
            forwards.pop(0)()
        multiply(t)
        if t:
            to_side(t - 1)
        for forward in forwards[max(t - 1, 0) * share : t * share] if pairs > 1 else forwards:
            forward()
    to_side(pairs - 1)
    to_far(0)
    order_queries()
    for t in range(1, pairs - 1):
        to_far(t)
    keys_complete()
    for chunk in range(chunks):
        attend(chunk)
        if chunk == 0 and pairs > 1:
            to_far(pairs - 1)

    total = own[lax.rem(far, subs)]
    for k in range(1, nz):
        sender = far_of(nz - k)
        arrived(far_recv.at[sender], f_rsem.at[sender])
        total = total + far_recv[sender].astype(jnp.float32)
    gate, up = total[:, :width], total[:, width:]
    hidden[far, side, core] = (gate / (1.0 + jnp.exp(-gate)) * up).astype(jnp.bfloat16)

    def pass_on(where, slot_side, ssems, rsems, device):
        here = hidden.at[where, slot_side, core]
        send(here, here, ssems, rsems, device)

    mine_block = hidden.at[far, side, core]
    for k in range(1, nz):
        send(mine_block, mine_block, hz_ssem.at[k], hz_rsem.at[far], at_far(far_of(k)))
    for k in range(nz):
        where = far_of(nz - k) if k else far
        if k:
            arrived(hidden.at[where, side, core], hz_rsem.at[where])
        pass_on(where, side, hx_ssem.at[k], hx_rsem.at[where], beside)
        pass_on(where, side, hc_ssem.at[0, k], hc_rsem.at[0, where], sibling)
    for k in range(nz):
        where = far_of(nz - k) if k else far
        arrived(hidden.at[where, 1 - side, core], hx_rsem.at[where])
        pass_on(where, 1 - side, hc_ssem.at[1, k], hc_rsem.at[1, where], sibling)

    for j in range(2):
        slot_side = side if j == 0 else 1 - side
        for d in range(pairs):
            expert = down_expert[d, j]
            pair = lax.rem(far // subs + d, pairs)
            for s in range(subs):
                where = pair * subs + s
                arrived(hidden.at[where, slot_side, 1 - core], hc_rsem.at[j, where])
            strips = []
            for c in range(2):
                for r in range(row_blocks):
                    strips.append(
                        jnp.concatenate(
                            [
                                hidden[pair * subs + q * row_blocks + r, slot_side, c]
                                for q in range(col_blocks)
                            ],
                            axis=1,
                        )
                    )
            down_copies[d, j].wait()
            made = lax.dot_general(
                jnp.concatenate(strips, axis=0),
                down_w[expert],
                (((1,), (1,)), ((), ())),
                preferred_element_type=jnp.float32,
            ).astype(jnp.bfloat16)
            for s in range(owners):
                result[s, pl.ds(pl.multiple_of(expert * CAP, CAP), CAP), :] = made[
                    s * CAP : (s + 1) * CAP
                ]

    def combine(k):
        weighted = weighted_of[k]
        high = weighted.astype(jnp.bfloat16)
        rest = weighted - high.astype(jnp.float32)
        middle = rest.astype(jnp.bfloat16)
        low = (rest - middle.astype(jnp.float32)).astype(jnp.bfloat16)
        rows_back = result[owner_of(k)]
        return sum(
            lax.dot_general(
                part, rows_back, (((0,), (0,)), ((), ())), preferred_element_type=jnp.float32
            )
            for part in (low, middle, high)
        )

    for k in range(1, owners):
        back_send[k] = combine(k)
        send(
            back_send.at[k], back_recv.at[exp], b_ssem.at[k], b_rsem.at[exp], (ctx, owner_of(k))
        )
    answer = combine(0)
    for k in range(1, owners):
        owner = owner_of(k)
        arrived(back_recv.at[owner], b_rsem.at[owner])
        answer = answer + back_recv[owner]
    out_ref[...] = answer.astype(out_ref.dtype)
    for copy in sent:
        copy.wait_send()

    @if_active
    def _():
        for copy in sent_active:
            copy.wait_send()


def layer(queries, latents, offsets, moe_input, routes, gate_values, w_gate, w_up, w_down):
    n, owners = lax.axis_size("ctx"), lax.axis_size("exp")
    held, depth, ff = w_gate.shape
    count, local_width = moe_input.shape
    half = owners * CAP // 2
    pairs = held // 2
    nz = n // 4
    subs = nz // pairs
    width = ff * (half // 16) // subs
    dma = pltpu.SemaphoreType.DMA
    bf16, f32 = jnp.bfloat16, jnp.float32
    vm = pltpu.VMEM
    scratch = [
        vm((16, 128), f32), vm((n * latents.shape[0], LAT + ROPE), bf16),
        dma((nz,)), dma((nz,)), dma((nz,)), dma((nz,)), dma((2, nz)), dma((2, nz)),
        dma((2, nz)), dma((2, nz)),
        vm((queries.shape[0] * H, LAT + ROPE), f32), vm((128, LAT), f32),
        vm((held, depth, ff), bf16), vm((held, depth, ff), bf16), vm((held, depth, ff), bf16),
        dma((3, pairs, 2)),
        vm((owners, 16, 128), f32), vm((owners, count, local_width), bf16),
        dma((2, owners)), dma((2, owners)),
        vm((held, owners * CAP, local_width), bf16),
        vm((pairs, 2, 2 * half, 2 * ff), f32), vm((pairs, 2, half, 2 * ff), bf16),
        vm((pairs, 2, half, 2 * ff), bf16), dma((pairs, 2)), dma((pairs, 2)),
        vm((pairs, half, 2 * ff), bf16), vm((pairs, half, 2 * ff), bf16), dma((pairs,)), dma((pairs,)),
        vm((pairs, subs, 16, 2 * width), bf16), vm((nz, 16, 2 * width), bf16),
        vm((subs, 16, 2 * width), f32), dma((pairs, subs)), dma((nz,)),
        vm((nz, 2, 2, 16, width), bf16),
        dma((nz,)), dma((nz,)), dma((nz,)), dma((nz,)), dma((2, nz)), dma((2, nz)),
        vm((owners, held * CAP, local_width), bf16),
        vm((owners, count, local_width), f32), vm((owners, count, local_width), f32),
        dma((owners,)), dma((owners,)),
    ]
    any_space = pl.BlockSpec(memory_space=pl.ANY)
    in_vmem = pl.BlockSpec(memory_space=pltpu.VMEM)
    return pl.pallas_call(
        functools.partial(expert_kernel, n, owners),
        out_shape=[
            jax.ShapeDtypeStruct((queries.shape[0], H * LAT), bf16),
            jax.ShapeDtypeStruct(moe_input.shape, bf16),
        ],
        in_specs=[
            pl.BlockSpec(memory_space=pltpu.SMEM), in_vmem, in_vmem, in_vmem, in_vmem, in_vmem,
            any_space, any_space, any_space,
        ],
        out_specs=[in_vmem, in_vmem],
        scratch_shapes=scratch,
        compiler_params=pltpu.CompilerParams(
            collective_id=0, has_side_effects=True, vmem_limit_bytes=56 * 2**20
        ),
        cost_estimate=pl.CostEstimate(
            flops=6 * held * owners * CAP * depth * ff,
            bytes_accessed=3 * held * depth * ff * 2,
            transcendentals=0,
        ),
        name="layer",
    )(
        offsets, queries, latents, routes.T, gate_values.T, moe_input,
        w_gate, w_up, jnp.swapaxes(w_down, 1, 2),
    )


def solution(mesh):
    return jax.shard_map(
        lambda *operands: tuple(layer(*operands)),
        mesh=mesh,
        in_specs=(
            P(("ctx", "exp"), None),
            P("ctx", None),
            P(("ctx", "exp")),
            P("exp", "ctx"),
            P("exp", None),
            P("exp", None),
            P("exp", "ctx", None),
            P("exp", "ctx", None),
            P("exp", None, "ctx"),
        ),
        out_specs=(P(("ctx", "exp"), None), P("exp", "ctx")),
        check_vma=False,
    )
```

```python
import functools

import jax
import jax.numpy as jnp
from jax import lax
from jax.experimental import pallas as pl
from jax.experimental.pallas import tpu as pltpu
from jax.sharding import PartitionSpec as P

H = 128
LAT = 512
ROPE = 64
TOPK = 6
EXPERTS = 16
CAP = 16
MESH = pl.DeviceIdType.MESH

softmax_scale = 192.0 ** (-0.5)


def expert_kernel(
    n, owners,
    offset_ref, query_ref, latent_ref, routes_ref, gates_ref, tokens_ref, gate_hbm, up_hbm, down_hbm,
    attention_ref, out_ref,
    table, keys, kz_ssem, kz_rsem, kx_ssem, kx_rsem, kc_ssem, kc_rsem, ordered, mixture,
    gate_w, up_w, down_w, w_sem,
    tables, tokens, t_ssem, t_rsem, x_rows,
    keep, core_send, core_recv, c_ssem, c_rsem,
    side_send, side_recv, s_ssem, s_rsem,
    far_send, far_recv, own, f_ssem, f_rsem,
    hidden, hz_ssem, hz_rsem, hx_ssem, hx_rsem, hc_ssem, hc_rsem,
    result, back_send, back_recv, b_ssem, b_rsem,
):
    held = gate_hbm.shape[0]
    ff = gate_hbm.shape[2]
    count = tokens_ref.shape[0]
    rows = owners * CAP
    half = rows // 2
    pairs = held // 2
    nz = n // 4
    subs = nz // pairs
    block_rows = latent_ref.shape[0]
    query_count = query_ref.shape[0]
    row_blocks = half // 16
    col_blocks = subs // row_blocks
    width = ff // col_blocks

    ctx = lax.axis_index("ctx")
    exp = lax.axis_index("exp")
    core = lax.rem(ctx, 2)
    side = lax.rem(ctx // 2, 2)
    far = ctx // 4
    sibling = (ctx + 1 - 2 * core, exp)
    beside = (ctx + 2 - 4 * side, exp)

    def at_far(index):
        return (index * 4 + side * 2 + core, exp)

    def far_of(step):
        return lax.rem(far + step, nz)

    def owner_of(step):
        return lax.rem(exp + step, owners)

    pair_of = [lax.rem(far // subs + 1 + i, pairs) for i in range(pairs)]
    weight_copies = {}
    for i in range(pairs):
        for j in range(2):
            expert = pair_of[i] * 2 + (1 - side if j == 0 else side)
            weight_copies[i, j] = [
                pltpu.make_async_copy(hbm.at[expert], vmem.at[expert], w_sem.at[k, i, j])
                for k, (hbm, vmem) in enumerate(((gate_hbm, gate_w), (up_hbm, up_w)))
            ]
    down_order = [(d, j) for d in range(pairs) for j in range(2)]
    down_expert = {}
    down_copies = {}
    for d, j in down_order:
        expert = lax.rem(far // subs + d, pairs) * 2 + (side if j == 0 else 1 - side)
        down_expert[d, j] = expert
        down_copies[d, j] = pltpu.make_async_copy(
            down_hbm.at[expert], down_w.at[expert], w_sem.at[2, d, j]
        )

    def start_weights(i):
        for j in range(2):
            for copy in weight_copies[i, j]:
                copy.start()

    for i in range(min(2, pairs)):
        start_weights(i)

    table[...] = jnp.zeros_like(table)
    table[:TOPK, :count] = routes_ref[...].astype(jnp.float32)
    table[8 : 8 + TOPK, :count] = gates_ref[...]

    barrier = pltpu.get_barrier_semaphore()
    greeted = [sibling, beside]
    greeted += [at_far(far_of(k)) for k in range(1, nz)]
    greeted += [(ctx, owner_of(k)) for k in range(1, owners)]
    for device in greeted:
        pl.semaphore_signal(barrier, inc=1, device_id=device, device_id_type=MESH)
    pl.semaphore_wait(barrier, len(greeted))

    sent = []

    def send(src, dst, ssem, rsem, device):
        copy = pltpu.make_async_remote_copy(
            src_ref=src, dst_ref=dst, send_sem=ssem, recv_sem=rsem,
            device_id=device, device_id_type=MESH,
        )
        copy.start()
        sent.append(copy)

    def arrived(dst, sem):
        pltpu.make_async_remote_copy(
            src_ref=dst, dst_ref=dst, send_sem=sem, recv_sem=sem,
            device_id=sibling, device_id_type=MESH,
        ).wait_recv()

    for k in range(1, owners):
        device = (ctx, owner_of(k))
        send(table, tables.at[exp], t_ssem.at[0, k], t_rsem.at[0, exp], device)
        send(tokens_ref, tokens.at[exp], t_ssem.at[1, k], t_rsem.at[1, exp], device)

    def keys_at(where, slot_side, slot_core):
        start = (where * 4 + slot_side * 2 + slot_core) * block_rows
        return keys.at[pl.ds(pl.multiple_of(start, 16), block_rows)]

    own_keys = keys_at(far, side, core)
    own_keys[...] = latent_ref[...]
    for k in range(1, nz):
        send(own_keys, own_keys, kz_ssem.at[k], kz_rsem.at[far], at_far(far_of(k)))

    def keys_here(k):
        where = far_of(nz - k) if k else far
        here = keys_at(where, side, core)
        if k:
            arrived(here, kz_rsem.at[where])
        send(here, here, kx_ssem.at[k], kx_rsem.at[where], beside)
        send(here, here, kc_ssem.at[0, k], kc_rsem.at[0, where], sibling)

    def keys_beside(k):
        where = far_of(nz - k) if k else far
        here = keys_at(where, 1 - side, core)
        arrived(here, kx_rsem.at[where])
        send(here, here, kc_ssem.at[1, k], kc_rsem.at[1, where], sibling)

    def keys_complete():
        for where in range(nz):
            for j in range(2):
                slot_side = side if j == 0 else 1 - side
                arrived(keys_at(where, slot_side, 1 - core), kc_rsem.at[j, where])

    keys_here(0)

    wide = 2 * (LAT + ROPE)
    pair_rows = 2 * query_count

    def order_queries():
        @pl.loop(0, H // 2, unroll=4)
        def _(at):
            two = query_ref[:, pl.ds(pl.multiple_of(at * wide, 128), wide)].astype(jnp.float32)
            ordered[pl.ds(pl.multiple_of(at * pair_rows, 8), pair_rows), :] = jnp.concatenate(
                [two[:, : LAT + ROPE], two[:, LAT + ROPE :]], axis=0
            )

    def attend(chunk):
        height = mixture.shape[0]
        scores = (
            lax.dot_general(
                ordered[chunk * height : (chunk + 1) * height, :].astype(jnp.bfloat16),
                keys[...],
                (((1,), (1,)), ((), ())),
                preferred_element_type=jnp.float32,
            )
            * softmax_scale
        )
        key_pos = lax.broadcasted_iota(jnp.int32, scores.shape, 1)
        query_pos = offset_ref[0] + lax.rem(
            lax.broadcasted_iota(jnp.int32, (height, 1), 0), query_count
        )
        scores = jnp.where(key_pos <= query_pos, scores, -jnp.inf)
        weights = jnp.exp(scores - jnp.max(scores, axis=1, keepdims=True))
        denominator = jnp.sum(weights, axis=1, keepdims=True)
        mixed = jnp.dot(
            weights.astype(jnp.bfloat16), keys[:, :LAT], preferred_element_type=jnp.float32
        )
        mixture[...] = mixed / denominator

        @pl.loop(0, height // pair_rows, unroll=4)
        def _(at):
            two = mixture[pl.ds(pl.multiple_of(at * pair_rows, 8), pair_rows), :]
            start = (chunk * (height // pair_rows) + at) * 2 * LAT
            for k in range(2):
                attention_ref[:, pl.ds(pl.multiple_of(start + k * LAT, 128), LAT)] = two[
                    k * query_count : (k + 1) * query_count
                ].astype(attention_ref.dtype)

    first = exp * held
    expert_ids = (lax.broadcasted_iota(jnp.int32, (held, count), 0) + first).astype(jnp.float32)
    earlier = (
        lax.broadcasted_iota(jnp.int32, (count, count), 0)
        < lax.broadcasted_iota(jnp.int32, (count, count), 1)
    ).astype(jnp.bfloat16)
    slots = lax.broadcasted_iota(jnp.int32, (held, CAP, count), 1).astype(jnp.float32)

    def placement(listed):
        named = jnp.zeros((held, count), jnp.float32)
        gates = jnp.zeros((held, count), jnp.float32)
        for k in range(TOPK):
            hit = listed[k : k + 1, :count] == expert_ids
            named = jnp.where(hit, 1.0, named)
            gates = jnp.where(hit, listed[8 + k : 9 + k, :count], gates)
        rank = jnp.dot(named.astype(jnp.bfloat16), earlier, preferred_element_type=jnp.float32)
        rank = jnp.where(named > 0.5, rank, -1.0)
        picked = rank[:, None, :] == slots
        chosen = jnp.where(picked, 1.0, 0.0).reshape(held * CAP, count)
        weighted = jnp.where(picked, gates[:, None, :], 0.0).reshape(held * CAP, count)
        return chosen.astype(jnp.bfloat16), weighted

    def place(listed, values, owner):
        chosen, weighted = placement(listed)
        placed = jnp.dot(chosen, values, preferred_element_type=jnp.float32).astype(jnp.bfloat16)
        for e in range(held):
            x_rows[e, pl.ds(pl.multiple_of(owner * CAP, CAP), CAP), :] = placed[e * CAP : (e + 1) * CAP]
        return weighted

    weighted_of = {0: place(table[...], tokens_ref[...], exp)}
    for k in range(1, owners):
        owner = owner_of(k)
        arrived(tables.at[owner], t_rsem.at[0, owner])
        arrived(tokens.at[owner], t_rsem.at[1, owner])
        weighted_of[k] = place(tables[owner], tokens[owner], owner)

    mine = pl.ds(pl.multiple_of(core * half, 16), half)
    other = pl.ds(pl.multiple_of((1 - core) * half, 16), half)

    def multiply(i):
        if i + 2 < pairs:
            start_weights(i + 2)
        if i == max(pairs - 2, 0):
            for key in down_order:
                down_copies[key].start()
        for j in range(2):
            expert = pair_of[i] * 2 + (1 - side if j == 0 else side)
            for k, weight in ((0, gate_w), (1, up_w)):
                weight_copies[i, j][k].wait()
                columns = slice(k * ff, (k + 1) * ff)
                keep[i, j, :, columns] = jnp.dot(
                    x_rows[expert], weight[expert], preferred_element_type=jnp.float32
                )
            core_send[i, j] = keep[i, j, other, :].astype(jnp.bfloat16)
            send(core_send.at[i, j], core_recv.at[i, j], c_ssem.at[i, j], c_rsem.at[i, j], sibling)

    def to_side(i):
        arrived(core_recv.at[i, 0], c_rsem.at[i, 0])
        side_send[i] = (keep[i, 0, mine, :] + core_recv[i, 0].astype(jnp.float32)).astype(jnp.bfloat16)
        send(side_send.at[i], side_recv.at[i], s_ssem.at[i], s_rsem.at[i], beside)

    def block(i, sub):
        row = lax.rem(sub, row_blocks)
        return i, row, sub // row_blocks

    def to_far(i):
        arrived(core_recv.at[i, 1], c_rsem.at[i, 1])
        arrived(side_recv.at[i], s_rsem.at[i])
        total = (
            keep[i, 1, mine, :] + core_recv[i, 1].astype(jnp.float32) + side_recv[i].astype(jnp.float32)
        )
        for r in range(row_blocks):
            for c in range(col_blocks):
                for k in range(2):
                    piece = total[r * 16 : r * 16 + 16, k * ff + c * width : k * ff + (c + 1) * width]
                    at = c * row_blocks + r
                    far_send[i, at, :, k * width : (k + 1) * width] = piece.astype(jnp.bfloat16)
                    if i == pairs - 1:
                        own[at, :, k * width : (k + 1) * width] = piece
        my_sub = lax.rem(far, subs)
        for s in range(subs if i < pairs - 1 else subs - 1):
            sub = lax.rem(my_sub + 1 + s, subs)
            dest = pair_of[i] * subs + sub
            send(
                far_send.at[i, sub], far_recv.at[far], f_ssem.at[i, s], f_rsem.at[far], at_far(dest)
            )

    forwards = [functools.partial(keys_here, k) for k in range(1, nz)]
    forwards += [functools.partial(keys_beside, k) for k in range(nz)]
    chunks = ordered.shape[0] // mixture.shape[0]
    share = -(-len(forwards) // max(pairs - 2, 1))
    for t in range(pairs):
        multiply(t)
        if t:
            to_side(t - 1)
        for forward in forwards[max(t - 2, 0) * share : max(t - 1, 0) * share] if pairs > 2 else forwards * (t == 0):
            forward()
    to_side(pairs - 1)
    to_far(0)
    order_queries()
    for t in range(1, pairs):
        to_far(t)
    keys_complete()
    for chunk in range(chunks // 2):
        attend(chunk)

    total = own[lax.rem(far, subs)]
    for k in range(1, nz):
        sender = far_of(nz - k)
        arrived(far_recv.at[sender], f_rsem.at[sender])
        total = total + far_recv[sender].astype(jnp.float32)
    gate, up = total[:, :width], total[:, width:]
    hidden[far, side, core] = (gate / (1.0 + jnp.exp(-gate)) * up).astype(jnp.bfloat16)

    def pass_on(where, slot_side, ssems, rsems, device):
        here = hidden.at[where, slot_side, core]
        send(here, here, ssems, rsems, device)

    mine_block = hidden.at[far, side, core]
    for k in range(1, nz):
        send(mine_block, mine_block, hz_ssem.at[k], hz_rsem.at[far], at_far(far_of(k)))
    attend(chunks // 2)
    for k in range(nz):
        where = far_of(nz - k) if k else far
        if k:
            arrived(hidden.at[where, side, core], hz_rsem.at[where])
        pass_on(where, side, hx_ssem.at[k], hx_rsem.at[where], beside)
        pass_on(where, side, hc_ssem.at[0, k], hc_rsem.at[0, where], sibling)
    for chunk in range(chunks // 2 + 1, chunks):
        attend(chunk)
    for k in range(nz):
        where = far_of(nz - k) if k else far
        arrived(hidden.at[where, 1 - side, core], hx_rsem.at[where])
        pass_on(where, 1 - side, hc_ssem.at[1, k], hc_rsem.at[1, where], sibling)

    for j in range(2):
        slot_side = side if j == 0 else 1 - side
        for d in range(pairs):
            expert = down_expert[d, j]
            pair = lax.rem(far // subs + d, pairs)
            for s in range(subs):
                where = pair * subs + s
                arrived(hidden.at[where, slot_side, 1 - core], hc_rsem.at[j, where])
            strips = []
            for c in range(2):
                for r in range(row_blocks):
                    strips.append(
                        jnp.concatenate(
                            [
                                hidden[pair * subs + q * row_blocks + r, slot_side, c]
                                for q in range(col_blocks)
                            ],
                            axis=1,
                        )
                    )
            down_copies[d, j].wait()
            made = lax.dot_general(
                jnp.concatenate(strips, axis=0),
                down_w[expert],
                (((1,), (1,)), ((), ())),
                preferred_element_type=jnp.float32,
            ).astype(jnp.bfloat16)
            for s in range(owners):
                result[s, pl.ds(pl.multiple_of(expert * CAP, CAP), CAP), :] = made[
                    s * CAP : (s + 1) * CAP
                ]

    def combine(k):
        weighted = weighted_of[k]
        high = weighted.astype(jnp.bfloat16)
        rest = weighted - high.astype(jnp.float32)
        middle = rest.astype(jnp.bfloat16)
        low = (rest - middle.astype(jnp.float32)).astype(jnp.bfloat16)
        rows_back = result[owner_of(k)]
        return sum(
            lax.dot_general(
                part, rows_back, (((0,), (0,)), ((), ())), preferred_element_type=jnp.float32
            )
            for part in (low, middle, high)
        )

    for k in range(1, owners):
        back_send[k] = combine(k)
        send(
            back_send.at[k], back_recv.at[exp], b_ssem.at[k], b_rsem.at[exp], (ctx, owner_of(k))
        )
    answer = combine(0)
    for k in range(1, owners):
        owner = owner_of(k)
        arrived(back_recv.at[owner], b_rsem.at[owner])
        answer = answer + back_recv[owner]
    out_ref[...] = answer.astype(out_ref.dtype)
    for copy in sent:
        copy.wait_send()


def layer(queries, latents, offsets, moe_input, routes, gate_values, w_gate, w_up, w_down):
    n, owners = lax.axis_size("ctx"), lax.axis_size("exp")
    held, depth, ff = w_gate.shape
    count, local_width = moe_input.shape
    half = owners * CAP // 2
    pairs = held // 2
    nz = n // 4
    subs = nz // pairs
    width = ff * (half // 16) // subs
    dma = pltpu.SemaphoreType.DMA
    bf16, f32 = jnp.bfloat16, jnp.float32
    vm = pltpu.VMEM
    scratch = [
        vm((16, 128), f32), vm((n * latents.shape[0], LAT + ROPE), bf16),
        dma((nz,)), dma((nz,)), dma((nz,)), dma((nz,)), dma((2, nz)), dma((2, nz)),
        vm((queries.shape[0] * H, LAT + ROPE), f32), vm((128, LAT), f32),
        vm((held, depth, ff), bf16), vm((held, depth, ff), bf16), vm((held, depth, ff), bf16),
        dma((3, pairs, 2)),
        vm((owners, 16, 128), f32), vm((owners, count, local_width), bf16),
        dma((2, owners)), dma((2, owners)),
        vm((held, owners * CAP, local_width), bf16),
        vm((pairs, 2, 2 * half, 2 * ff), f32), vm((pairs, 2, half, 2 * ff), bf16),
        vm((pairs, 2, half, 2 * ff), bf16), dma((pairs, 2)), dma((pairs, 2)),
        vm((pairs, half, 2 * ff), bf16), vm((pairs, half, 2 * ff), bf16), dma((pairs,)), dma((pairs,)),
        vm((pairs, subs, 16, 2 * width), bf16), vm((nz, 16, 2 * width), bf16),
        vm((subs, 16, 2 * width), f32), dma((pairs, subs)), dma((nz,)),
        vm((nz, 2, 2, 16, width), bf16),
        dma((nz,)), dma((nz,)), dma((nz,)), dma((nz,)), dma((2, nz)), dma((2, nz)),
        vm((owners, held * CAP, local_width), bf16),
        vm((owners, count, local_width), f32), vm((owners, count, local_width), f32),
        dma((owners,)), dma((owners,)),
    ]
    any_space = pl.BlockSpec(memory_space=pl.ANY)
    in_vmem = pl.BlockSpec(memory_space=pltpu.VMEM)
    return pl.pallas_call(
        functools.partial(expert_kernel, n, owners),
        out_shape=[
            jax.ShapeDtypeStruct((queries.shape[0], H * LAT), bf16),
            jax.ShapeDtypeStruct(moe_input.shape, bf16),
        ],
        in_specs=[
            pl.BlockSpec(memory_space=pltpu.SMEM), in_vmem, in_vmem, in_vmem, in_vmem, in_vmem,
            any_space, any_space, any_space,
        ],
        out_specs=[in_vmem, in_vmem],
        scratch_shapes=scratch,
        compiler_params=pltpu.CompilerParams(
            collective_id=0, has_side_effects=True, vmem_limit_bytes=56 * 2**20
        ),
        cost_estimate=pl.CostEstimate(
            flops=6 * held * owners * CAP * depth * ff,
            bytes_accessed=3 * held * depth * ff * 2,
            transcendentals=0,
        ),
        name="layer",
    )(
        offsets, queries, latents, routes.T, gate_values.T, moe_input,
        w_gate, w_up, jnp.swapaxes(w_down, 1, 2),
    )


def solution(mesh):
    return jax.shard_map(
        lambda *operands: tuple(layer(*operands)),
        mesh=mesh,
        in_specs=(
            P(("ctx", "exp"), None),
            P("ctx", None),
            P(("ctx", "exp")),
            P("exp", "ctx"),
            P("exp", None),
            P("exp", None),
            P("exp", "ctx", None),
            P("exp", "ctx", None),
            P("exp", None, "ctx"),
        ),
        out_specs=(P(("ctx", "exp"), None), P("exp", "ctx")),
        check_vma=False,
    )
```
